32 devices in a mesh: frames: 8 (over z, x), cols: 4 (over y, core).
Axes of the slice: x: 2, y: 2, z: 4, core: 2. Of those that a mesh axis runs over, the one named last changes fastest.
Arguments:
- right_side: float32 [6, 8192], P(None, ('frames', 'cols')), may hold values from -6 to 6
- diag_blocks: float32 [6, 6, 8192], P(None, None, ('frames', 'cols')), may hold values from -0.6 to 24, as said below
- band_blocks: float32 [8, 6, 6, 8192], P(None, None, None, ('frames', 'cols')), may hold values from -0.6 to 0.6
- reach: int32 [8192], P(('frames', 'cols')), may hold values from 1 to 8
- tiles: float32 [8, 4, 8, 384, 384], P('frames', 'cols'), may hold values from -0.09185587 to 0.09185587
- tile_rows: int32 [8, 4, 8], P('frames', 'cols'), may hold values from 0 to 15
- tile_cols: int32 [8, 4, 8], P('frames', 'cols'), may hold values from 0 to 31
- tile_count: int32 [8, 4], P('frames', 'cols'), may hold values from 1 to 8
Outputs:
- solution: float32 [6, 8192], P(None, ('frames', 'cols'))
- residual: float32 [6, 8192], P(None, ('frames', 'cols'))
The draws below stay inside these ranges and needn't reach their ends.
Inputs may be any that keep to these rules, and one draw needn't show every extreme that they name: `diag_blocks`: each block is symmetric, with diagonal entries at least 6 and larger than the sum of its other entries' magnitudes in that row, so each block is positive definite.
All inputs are finite; a program needn't handle non-finite values.
Results may differ from the reference program's by a relative error of at most 0.0003.
Values sent between devices are 32-bit elements; how exact they have to be, the bound alone decides.
A program may use at most 64 MiB of HBM per device.

```python
import jax
import jax.numpy as jnp
from jax import lax

FR_DEV = 256
BAND = 8
TF = 64
TILES_DEV = 8
ITERS = 4
TILE = 384
KEYFRAMES = 8192
ROW_TILES = 16
COL_TILES = 32
N_FRAMES = 8
N_COLS = 4


def draw_diag_blocks(key, part):
    key_a, key_b = jax.random.split(jax.random.fold_in(key, 11))
    level_diag = jax.random.uniform(key_a, (6, KEYFRAMES), jnp.float32, 6.0, 12.0)
    noise_part = jnp.clip(0.15 * jax.random.normal(key_b, (6, 6, KEYFRAMES), jnp.float32), -0.3, 0.3)
    symmetric = noise_part + jnp.transpose(noise_part, (1, 0, 2))
    identity = jnp.eye(6, dtype=jnp.float32)[:, :, None]
    return symmetric * (1.0 - identity) + identity * level_diag[:, None, :]


def with_ends(values, stream_key, least, largest):
    spot = [jax.random.randint(jax.random.fold_in(stream_key, axis), (), 0, length) for axis, length in enumerate(values.shape)]
    longest = values.shape.index(max(values.shape))
    next_to = spot[:longest] + [(spot[longest] + 1) % values.shape[longest]] + spot[longest + 1:]
    return values.at[tuple(spot)].set(least).at[tuple(next_to)].set(largest)


def block_scale(key, shape, cuts, least, top_value):
    gain = 1.0
    for axis_at, blocks in cuts:
        heights = jax.random.uniform(jax.random.fold_in(jax.random.fold_in(key, 6), axis_at), (blocks,), jnp.float32, least / len(cuts), top_value / len(cuts))
        gain = gain * jnp.repeat(jnp.exp(heights), shape[axis_at] // blocks).reshape((-1,) + (1,) * (len(shape) - 1 - axis_at))
    return gain


def bell_draw(stream_key, shape, width, most, pieces=(), kind=jnp.bfloat16):
    entries = width * jax.random.normal(stream_key, shape, jnp.float32)
    if pieces:
        entries = entries * block_scale(stream_key, shape, pieces, -0.22, 0.18)
    return jnp.clip(entries, -most, most).astype(kind)


def setup_inputs(seed: int = 0) -> dict:
    keys = jax.random.split(jax.random.key(seed), 9)
    right_side = bell_draw(keys[0], (6, KEYFRAMES), 1.0, 6.0, ((1, 32),), jnp.float32)
    diag_blocks = draw_diag_blocks(jax.random.fold_in(keys[8], 71), 0)
    band_blocks = bell_draw(keys[2], (BAND, 6, 6, KEYFRAMES), 0.1, 0.6, ((3, 32),), jnp.float32)
    reach = with_ends(jax.random.randint(keys[3], (KEYFRAMES,), 1, BAND + 1), jax.random.fold_in(keys[3], 1), 1, BAND).astype(jnp.int32)
    tiles = bell_draw(keys[4], (N_FRAMES, N_COLS, TILES_DEV, TILE, TILE), (0.3 / TILE ** 0.5), 0.09185587, ((0, 8), (1, 4)), jnp.float32)
    tile_rows = with_ends(jax.random.randint(keys[5], (N_FRAMES, N_COLS, TILES_DEV), 0, ROW_TILES), jax.random.fold_in(keys[5], 1), 0, ROW_TILES - 1).astype(jnp.int32)
    tile_cols = with_ends(jax.random.randint(keys[6], (N_FRAMES, N_COLS, TILES_DEV), 0, COL_TILES), jax.random.fold_in(keys[6], 1), 0, COL_TILES - 1).astype(jnp.int32)
    tile_count = with_ends(jax.random.randint(keys[7], (N_FRAMES, N_COLS), 1, TILES_DEV + 1), jax.random.fold_in(keys[7], 1), 1, TILES_DEV).astype(jnp.int32)
    return dict(right_side=right_side, diag_blocks=diag_blocks, band_blocks=band_blocks, reach=reach, tiles=tiles, tile_rows=tile_rows, tile_cols=tile_cols, tile_count=tile_count)


def invert_blocks(blocks):
    matrix_rows = [blocks[row_id] for row_id in range(6)]
    inverse = [jnp.zeros_like(blocks[0]).at[row_id].set(1.0) for row_id in range(6)]
    for pivot_id in range(6):
        pivot_value = matrix_rows[pivot_id][pivot_id]
        matrix_rows[pivot_id] = matrix_rows[pivot_id] / pivot_value
        inverse[pivot_id] = inverse[pivot_id] / pivot_value
        for row_id in range(6):
            if row_id != pivot_id:
                factor = matrix_rows[row_id][pivot_id]
                matrix_rows[row_id] = matrix_rows[row_id] - factor * matrix_rows[pivot_id]
                inverse[row_id] = inverse[row_id] - factor * inverse[pivot_id]
    return jnp.stack(inverse)


def precondition(inverse, vector):
    return jnp.einsum("abk,bk->ak", inverse, vector, precision=lax.Precision.HIGHEST)


def band_apply(vector, band_blocks, reach):
    frame_total = vector.shape[1]
    offsets = jnp.arange(1, BAND + 1, dtype=jnp.int32)
    frame_ids = jnp.arange(frame_total, dtype=jnp.int32)
    keep_mask = ((offsets[:, None] <= reach[None, :]) & (frame_ids[None, :] + offsets[:, None] < frame_total)).astype(jnp.float32)
    masked = band_blocks * keep_mask[:, None, None, :]
    padded = jnp.pad(vector, ((0, 0), (0, BAND)))
    result = jnp.zeros_like(vector)
    for offset in range(1, BAND + 1):
        blocks_now = masked[offset - 1]
        result = result + jnp.einsum("abk,bk->ak", blocks_now, padded[:, offset:offset + frame_total], precision=lax.Precision.HIGHEST)
        back_term = jnp.einsum("abk,ak->bk", blocks_now, vector, precision=lax.Precision.HIGHEST)
        result = result.at[:, offset:].add(back_term[:, :frame_total - offset])
    return result


def loop_apply(vector, tiles, tile_rows, tile_cols, tile_count):
    frame_groups, col_groups, slot_total = tile_rows.shape
    total_slots = frame_groups * col_groups * slot_total
    flat_tiles = tiles.reshape(total_slots, TILE, TILE)
    slot_index = jnp.arange(total_slots, dtype=jnp.int32)
    group_id = slot_index // slot_total
    slot_id = slot_index % slot_total
    frame_group = group_id // col_groups
    col_group = group_id % col_groups
    live_flag = (slot_id < tile_count.reshape(-1)[group_id]).astype(jnp.float32)
    row_start = (frame_group * col_groups * FR_DEV + tile_rows.reshape(-1) * TF).astype(jnp.int32)
    col_mid = tile_cols.reshape(-1) * TF
    col_start = (((col_mid // FR_DEV) * col_groups + col_group) * FR_DEV + col_mid % FR_DEV).astype(jnp.int32)

    def one_tile(totals, item):
        tile_now, row_at, col_at, alive_flag = item
        row_part = lax.dynamic_slice_in_dim(vector, row_at, TF, 1).reshape(-1)
        col_part = lax.dynamic_slice_in_dim(vector, col_at, TF, 1).reshape(-1)
        gain_row = (jnp.dot(tile_now, col_part, precision=lax.Precision.HIGHEST) * alive_flag).reshape(6, TF)
        gain_col = (jnp.dot(row_part, tile_now, precision=lax.Precision.HIGHEST) * alive_flag).reshape(6, TF)
        totals = lax.dynamic_update_slice_in_dim(totals, lax.dynamic_slice_in_dim(totals, row_at, TF, 1) + gain_row, row_at, 1)
        totals = lax.dynamic_update_slice_in_dim(totals, lax.dynamic_slice_in_dim(totals, col_at, TF, 1) + gain_col, col_at, 1)
        return totals, None

    result, unused = lax.scan(one_tile, jnp.zeros_like(vector), (flat_tiles, row_start, col_start, live_flag))
    return result


def reference(right_side, diag_blocks, band_blocks, reach, tiles, tile_rows, tile_cols, tile_count):
    inverse = invert_blocks(diag_blocks)

    def apply_system(vector):
        result = jnp.einsum("abk,bk->ak", diag_blocks, vector, precision=lax.Precision.HIGHEST)
        result = result + band_apply(vector, band_blocks, reach)
        return result + loop_apply(vector, tiles, tile_rows, tile_cols, tile_count)

    solution = jnp.zeros_like(right_side)
    residual = right_side
    precond = precondition(inverse, residual)
    direction = precond
    rz_now = jnp.sum(residual * precond)
    for iteration in range(ITERS):
        image_now = apply_system(direction)
        alpha_now = rz_now / jnp.sum(direction * image_now)
        solution = solution + alpha_now * direction
        residual = residual - alpha_now * image_now
        if iteration + 1 < ITERS:
            precond = precondition(inverse, residual)
            rz_next = jnp.sum(residual * precond)
            direction = precond + (rz_next / rz_now) * direction
            rz_now = rz_next
    return solution, residual
```

```python
import functools

import jax
import jax.numpy as jnp
from jax import lax
from jax.experimental import pallas as pl
from jax.experimental.pallas import tpu as pltpu
from jax.sharding import PartitionSpec as P

ITERS = 4
COMP = 6
SUB = 8
MESH = pl.DeviceIdType.MESH
HIGH = lax.Precision.HIGHEST


def swap_pairs(block, side):
    row = lax.broadcasted_iota(jnp.int32, block.shape, 0)
    lane = lax.broadcasted_iota(jnp.int32, block.shape, 1)
    odd = row % 2
    turned = pltpu.roll(block, side, 1)
    above = pltpu.roll(turned, SUB - 1, 0)
    below = pltpu.roll(turned, 1, 0)
    return jnp.where(odd == lane // side, block, jnp.where(odd == 0, above, below))


def kernel(
    nf,
    nc,
    rhs_ref,
    diag_ref,
    band_ref,
    reach_ref,
    tiles_hbm,
    rows_ref,
    cols_ref,
    count_ref,
    sol_ref,
    res_ref,
    tiles,
    band,
    inv,
    vecs,
    ys,
    row_in,
    col_in,
    halo_in,
    spill_out,
    spill_in,
    row_out,
    col_out,
    row_back,
    col_back,
    last_out,
    last_in,
    pick_row,
    pick_col,
    put_row,
    put_col,
    r_cols,
    c_rows,
    g_cols,
    col_acc,
    nus,
    tile_sem,
    s_row,
    r_row,
    s_col,
    r_col,
    s_halo,
    r_halo,
    s_spill,
    r_spill,
    s_rowb,
    r_rowb,
    s_colb,
    r_colb,
    s_last,
    r_last,
):
    f = lax.axis_index("frames")
    c = lax.axis_index("cols")
    slots, tile, _ = tiles.shape
    side = tile // COMP
    lanes = 2 * side
    chunks = tile // lanes
    blocks = vecs.shape[1]
    frames = blocks * lanes
    slab = blocks * SUB
    reach_len = band_ref.shape[0]

    load = pltpu.make_async_copy(tiles_hbm.at[0, 0], tiles, tile_sem)
    load.start()

    row_peers = [(f, lax.rem(c + d, nc)) for d in range(1, nc)]
    col_peers = [(lax.rem(f + d, nf), c) for d in range(1, nf)]
    after = (lax.rem(f + (c + 1) // nc, nf), lax.rem(c + 1, nc))
    before = (lax.rem(f + nf - 1 + (c + nc - 1) // nc, nf), lax.rem(c + nc - 1, nc))
    greet = row_peers + col_peers + [after, before]
    barrier = pltpu.get_barrier_semaphore()
    for peer in greet:
        pl.semaphore_signal(barrier, inc=1, device_id=peer, device_id_type=MESH)

    row_iota = lax.broadcasted_iota(jnp.int32, (SUB, lanes), 0)
    lane_iota = lax.broadcasted_iota(jnp.int32, (SUB, lanes), 1)
    zero = jnp.zeros((SUB, lanes), jnp.float32)

    ys[0] = jnp.zeros((blocks, SUB, lanes), jnp.float32)
    inv[...] = jnp.zeros_like(inv)
    band[...] = jnp.zeros_like(band)
    for h in range(blocks):
        cut = slice(h * lanes, (h + 1) * lanes)
        ys[0, h, 0:COMP, :] = rhs_ref[:, cut]
        for a in range(COMP):
            inv[a, h, 0:COMP, :] = diag_ref[a, :, cut]
    for h in range(blocks):
        mat = [inv[a, h] for a in range(COMP)]
        out = [jnp.where(row_iota == a, 1.0, 0.0) for a in range(COMP)]
        for p in range(COMP):
            pivot = mat[p][p : p + 1, :]
            mat[p] = mat[p] / pivot
            out[p] = out[p] / pivot
            for a in range(COMP):
                if a != p:
                    factor = mat[a][p : p + 1, :]
                    mat[a] = mat[a] - factor * mat[p]
                    out[a] = out[a] - factor * out[p]
        for a in range(COMP):
            inv[a, h] = out[a]

    def precondition(h, value):
        total = zero
        for a in range(COMP):
            total = total + inv[a, h] * value[a : a + 1, :]
        return total

    for h in range(blocks):
        vecs[0, h] = precondition(h, ys[0, h])

    ends = (f == nf - 1) & (c == nc - 1)
    limit = jnp.where(ends, frames, frames + reach_len)
    for h in range(blocks):
        cut = slice(h * lanes, (h + 1) * lanes)
        reach = reach_ref[:, cut]
        at = lax.broadcasted_iota(jnp.int32, (1, lanes), 1) + h * lanes
        for o in range(1, reach_len + 1):
            keep = jnp.where((o <= reach) & (at + o < limit), 1.0, 0.0)
            for a in range(COMP):
                band[o - 1, a, h, 0:COMP, :] = band_ref[o - 1, a, :, cut] * keep

    count = count_ref[0, 0]

    def targets(ids_ref, iota, width):
        out = jnp.full(iota.shape, -1, jnp.int32)
        slot_at = iota // width
        for s in range(slots):
            at = ids_ref[0, 0, s]
            base = jnp.where(s < count, (at // 2) * SUB + lax.rem(at, 2), -slab * nf * nc)
            for j in range(chunks):
                out = jnp.where(slot_at == j * slots + s, base + 2 * j, out)
        return out

    for ids, pick, put, width in ((rows_ref, pick_row, put_row, 1), (cols_ref, pick_col, put_col, SUB)):
        many = pick.shape[1]
        down = targets(ids, lax.broadcasted_iota(jnp.int32, (pick.shape[0], 1), 0), 1)
        pick[...] = jnp.where(lax.broadcasted_iota(jnp.int32, pick.shape, 1) == down, 1.0, 0.0)
        along = targets(ids, lax.broadcasted_iota(jnp.int32, (1, put.shape[1]), 1), width)
        put[...] = jnp.where(lax.broadcasted_iota(jnp.int32, put.shape, 0) == along, 1.0, 0.0)

    pl.semaphore_wait(barrier, len(greet))

    def remote(src, dst, send, recv, peer):
        copy = pltpu.make_async_remote_copy(
            src_ref=src, dst_ref=dst, send_sem=send, recv_sem=recv, device_id=peer, device_id_type=MESH
        )
        copy.start()
        return copy

    def step(k, carry):
        prev = jnp.maximum(k - 1, 0)
        v = [vecs[k, h] for h in range(blocks)]
        even = jnp.zeros((1, lanes), jnp.float32)
        odd = jnp.zeros((1, lanes), jnp.float32)
        for h in range(blocks):
            y = ys[k, h]
            even = even + jnp.sum(v[h] * y, axis=0, keepdims=True)
            odd = odd + jnp.sum(vecs[prev, h] * y, axis=0, keepdims=True)
        paired = [swap_pairs(v[h], side) for h in range(blocks)]
        paired[0] = jnp.where(row_iota == COMP, even, jnp.where(row_iota == COMP + 1, odd, paired[0]))
        for h in range(blocks):
            row_in[k, c, h * SUB : (h + 1) * SUB, :] = paired[h]
            col_in[k, f, h * SUB : (h + 1) * SUB, :] = paired[h]
        gathers = []
        for d in range(1, nf):
            gathers.append(remote(col_in.at[k, f], col_in.at[k, f], s_col.at[k, d], r_col.at[k, d], col_peers[d - 1]))
        for d in range(1, nc):
            gathers.append(remote(row_in.at[k, c], row_in.at[k, c], s_row.at[k, d], r_row.at[k, d], row_peers[d - 1]))
        halo = remote(vecs.at[k, 0], halo_in.at[k], s_halo.at[k], r_halo.at[k], before)

        image = [zero] * blocks
        spill = zero
        for o in range(1, reach_len + 1):
            passed = zero
            for h in range(blocks):
                term = zero
                for a in range(COMP):
                    term = term + band[o - 1, a, h] * v[h][a : a + 1, :]
                turned = pltpu.roll(term, o, 1)
                image[h] = image[h] + jnp.where(lane_iota >= o, turned, passed)
                passed = turned
            spill = spill + jnp.where(lane_iota < o, passed, 0.0)
        spill_out[k] = spill
        spilled = remote(spill_out.at[k], spill_in.at[k], s_spill.at[k], r_spill.at[k], after)

        halo.wait_recv()
        ext = v + [halo_in[k]]
        forward = [[zero] * COMP for _ in range(blocks)]
        for o in range(1, reach_len + 1):
            turned = [pltpu.roll(part, lanes - o, 1) for part in ext]
            for h in range(blocks):
                moved = jnp.where(lane_iota < lanes - o, turned[h], turned[h + 1])
                for a in range(COMP):
                    forward[h][a] = forward[h][a] + band[o - 1, a, h] * moved
        quad = jnp.zeros((1, lanes), jnp.float32)
        for h in range(blocks):
            ahead = zero
            for a in range(COMP):
                ahead = jnp.where(row_iota == a, jnp.sum(forward[h][a], axis=0, keepdims=True), ahead)
            quad = quad + jnp.sum(ahead * v[h], axis=0, keepdims=True)
            image[h] = image[h] + ahead

        for copy in gathers:
            copy.wait_recv()
        rows_all = row_in[k].reshape(nc * slab, lanes)
        cols_all = col_in[k].reshape(nf * slab, lanes)
        r_cols[...] = jnp.dot(pick_row[...], rows_all, precision=HIGH, preferred_element_type=jnp.float32).T
        c_rows[...] = jnp.dot(pick_col[...], cols_all, precision=HIGH, preferred_element_type=jnp.float32)

        @pl.when(k == 0)
        def _():
            load.wait()

        def strip(i, accs):
            accs = list(accs)
            at = pl.multiple_of(i * SUB, SUB)
            r_now = r_cols[pl.ds(at, SUB), :]
            g_now = zero
            for s in range(slots):
                for j in range(chunks):
                    col = j * slots + s
                    spot = pl.multiple_of(j * lanes + at, SUB)
                    x = jnp.broadcast_to(r_now[:, col : col + 1], (SUB, lanes))
                    dots = zero
                    for n in range(chunks):
                        part = tiles[s, pl.ds(spot, SUB), n * lanes : (n + 1) * lanes]
                        here = n * slots + s
                        dots = dots + part * c_rows[here : here + 1, :]
                        accs[here] = accs[here] + part * x
                    g_now = jnp.where(lane_iota == col, jnp.sum(dots, axis=1, keepdims=True), g_now)
            g_cols[pl.ds(at, SUB), :] = g_now
            return tuple(accs)

        accs = lax.fori_loop(0, lanes // SUB, strip, (zero,) * (slots * chunks))
        for q in range(slots * chunks):
            col_acc[q * SUB : (q + 1) * SUB, :] = accs[q]
        gains = g_cols[...]
        quad = 2.0 * (quad + jnp.sum(gains * r_cols[...], axis=0, keepdims=True))
        row_out[k] = jnp.dot(put_row[...], gains.T, precision=HIGH, preferred_element_type=jnp.float32)
        col_out[k] = jnp.dot(put_col[...], col_acc[...], precision=HIGH, preferred_element_type=jnp.float32)
        sums = jnp.zeros((2, lanes), jnp.float32)
        for d in range(nc):
            sums = sums + row_in[k, d, COMP:SUB, :]
        for d in range(nf):
            col_out[k, d * slab + COMP : d * slab + SUB, :] = sums
        for d in range(nc):
            spot = (d + 1) * slab - SUB + COMP
            row_out[k, spot : spot + 1, :] = quad
        backs = []
        for d in range(1, nf):
            peer = col_peers[d - 1]
            part = col_out.at[k, pl.ds(pl.multiple_of(peer[0] * slab, SUB), slab), :]
            backs.append(remote(part, col_back.at[k, f], s_colb.at[k, d], r_colb.at[k, d], peer))
        for d in range(1, nc):
            peer = row_peers[d - 1]
            part = row_out.at[k, pl.ds(pl.multiple_of(peer[1] * slab, SUB), slab), :]
            backs.append(remote(part, row_back.at[k, c], s_rowb.at[k, d], r_rowb.at[k, d], peer))
        col_back[k, f] = col_out[k, pl.ds(pl.multiple_of(f * slab, SUB), slab), :]
        row_back[k, c] = row_out[k, pl.ds(pl.multiple_of(c * slab, SUB), slab), :]
        spilled.wait_recv()
        image[0] = image[0] + spill_in[k]
        for copy in backs:
            copy.wait_recv()
        total = jnp.sum(row_back[k], axis=0) + jnp.sum(col_back[k], axis=0)
        nus[k] = total
        for h in range(blocks):
            part = jnp.where(row_iota < COMP, total[h * SUB : (h + 1) * SUB, :], 0.0)
            image[h] = image[h] + swap_pairs(part, side)
            ys[k + 1, h] = image[h]
            vecs[k + 1, h] = precondition(h, image[h])
        for copy in gathers + [halo, spilled] + backs:
            copy.wait_send()
        return carry

    lax.fori_loop(0, ITERS, step, 0)

    last = ITERS - 1
    last_out[...] = nus[last, slab - SUB : slab, :]
    finals = []
    for d in range(1, nf):
        finals.append(remote(last_out, last_in.at[f], s_last.at[d], r_last.at[d], col_peers[d - 1]))
    last_in[f] = last_out[...]

    moments = []
    for k in range(ITERS):
        if k:
            moments.append(jnp.sum(nus[k, COMP + 1 : COMP + 2, :], axis=1, keepdims=True))
        moments.append(jnp.sum(nus[k, COMP : COMP + 1, :], axis=1, keepdims=True))

    def quadratic(coefs, values):
        sums = {}
        for i, left in enumerate(coefs):
            for j, right in enumerate(coefs):
                sums.setdefault(i + j, []).append(left * right)
        total = None
        for at, terms in sums.items():
            term = sum(terms[1:], terms[0]) * values(at)
            total = term if total is None else total + term
        return total

    one = jnp.ones((1, 1), jnp.float32)
    none = jnp.zeros((1, 1), jnp.float32)
    rho = [one]
    pi = [one]
    xi = []
    gamma = quadratic(rho, lambda at: moments[at])
    for iteration in range(ITERS):
        if iteration == last:
            for copy in finals:
                copy.wait_recv()
            ending = jnp.sum(last_in[...], axis=0)[COMP : COMP + 1, :]
            moments.append(jnp.sum(ending, axis=1, keepdims=True))
        alpha = gamma / quadratic(pi, lambda at: moments[at] + moments[at + 1])
        xi = [x + alpha * p for x, p in zip(xi + [none] * (len(pi) - len(xi)), pi)]
        image = [(pi[i] if i < len(pi) else none) + (pi[i - 1] if i else none) for i in range(len(pi) + 1)]
        rho = [r - alpha * s for r, s in zip(rho + [none], image)]
        if iteration < last:
            fresh = quadratic(rho, lambda at: moments[at])
            beta = fresh / gamma
            pi = [r + beta * p for r, p in zip(rho, pi + [none])]
            gamma = fresh

    for h in range(blocks):
        cut = slice(h * lanes, (h + 1) * lanes)
        sol = zero
        res = zero
        for k in range(ITERS):
            sol = sol + xi[k] * vecs[k, h]
        for k in range(ITERS + 1):
            res = res + rho[k] * ys[k, h]
        sol_ref[:, cut] = sol[0:COMP, :]
        res_ref[:, cut] = res[0:COMP, :]
    for copy in finals:
        copy.wait_send()


def per_device(nf, nc, right_side, diag_blocks, band_blocks, reach, tiles, tile_rows, tile_cols, tile_count):
    slots, tile = tiles.shape[2], tiles.shape[3]
    lanes = 2 * (tile // COMP)
    chunks = tile // lanes
    frames = right_side.shape[1]
    blocks = frames // lanes
    slab = blocks * SUB
    reach_len = band_blocks.shape[0]
    padded = -(-slots * chunks // lanes) * lanes
    f32 = jnp.float32
    vmem = pl.BlockSpec(memory_space=pltpu.VMEM)
    smem = pl.BlockSpec(memory_space=pltpu.SMEM)
    dma = pltpu.SemaphoreType.DMA
    scratch = [
        pltpu.VMEM((slots, tile, tile), f32),
        pltpu.VMEM((reach_len, COMP, blocks, SUB, lanes), f32),
        pltpu.VMEM((COMP, blocks, SUB, lanes), f32),
        pltpu.VMEM((ITERS + 1, blocks, SUB, lanes), f32),
        pltpu.VMEM((ITERS + 1, blocks, SUB, lanes), f32),
        pltpu.VMEM((ITERS, nc, slab, lanes), f32),
        pltpu.VMEM((ITERS, nf, slab, lanes), f32),
        pltpu.VMEM((ITERS, SUB, lanes), f32),
        pltpu.VMEM((ITERS, SUB, lanes), f32),
        pltpu.VMEM((ITERS, SUB, lanes), f32),
        pltpu.VMEM((ITERS, nc * slab, lanes), f32),
        pltpu.VMEM((ITERS, nf * slab, lanes), f32),
        pltpu.VMEM((ITERS, nc, slab, lanes), f32),
        pltpu.VMEM((ITERS, nf, slab, lanes), f32),
        pltpu.VMEM((SUB, lanes), f32),
        pltpu.VMEM((nf, SUB, lanes), f32),
        pltpu.VMEM((padded, nc * slab), f32),
        pltpu.VMEM((padded, nf * slab), f32),
        pltpu.VMEM((nc * slab, padded), f32),
        pltpu.VMEM((nf * slab, slots * chunks * SUB), f32),
        pltpu.VMEM((lanes, padded), f32),
        pltpu.VMEM((padded, lanes), f32),
        pltpu.VMEM((lanes, padded), f32),
        pltpu.VMEM((slots * chunks * SUB, lanes), f32),
        pltpu.VMEM((ITERS, slab, lanes), f32),
        dma,
    ]
    for shape in ((ITERS, nc), (ITERS, nf), (ITERS,), (ITERS,), (ITERS, nc), (ITERS, nf), (nf,)):
        scratch += [dma(shape), dma(shape)]
    return pl.pallas_call(
        functools.partial(kernel, nf, nc),
        out_shape=(jax.ShapeDtypeStruct(right_side.shape, f32), jax.ShapeDtypeStruct(right_side.shape, f32)),
        in_specs=[vmem, vmem, vmem, vmem, pl.BlockSpec(memory_space=pl.ANY), smem, smem, smem],
        out_specs=(vmem, vmem),
        scratch_shapes=scratch,
        compiler_params=pltpu.CompilerParams(
            collective_id=0, has_side_effects=True, vmem_limit_bytes=32 * 1024 * 1024
        ),
        cost_estimate=pl.CostEstimate(
            flops=4 * ITERS * tiles.size, bytes_accessed=4 * (tiles.size + band_blocks.size), transcendentals=0
        ),
    )(right_side, diag_blocks, band_blocks, reach.reshape(1, -1), tiles, tile_rows, tile_cols, tile_count)


def solution(mesh):
    return jax.shard_map(
        functools.partial(per_device, mesh.shape["frames"], mesh.shape["cols"]),
        mesh=mesh,
        in_specs=(
            P(None, ("frames", "cols")),
            P(None, None, ("frames", "cols")),
            P(None, None, None, ("frames", "cols")),
            P(("frames", "cols")),
            P("frames", "cols", None, None, None),
            P("frames", "cols", None),
            P("frames", "cols", None),
            P("frames", "cols"),
        ),
        out_specs=(P(None, ("frames", "cols")), P(None, ("frames", "cols"))),
        check_vma=False,
    )
```

```python
import functools

import jax
import jax.numpy as jnp
from jax import lax
from jax.experimental import pallas as pl
from jax.experimental.pallas import tpu as pltpu
from jax.sharding import PartitionSpec as P

ITERS = 4
COMP = 6
SUB = 8
UNROLL = 4
MESH = pl.DeviceIdType.MESH


def swap_pairs(block, side):
    row = lax.broadcasted_iota(jnp.int32, block.shape, 0)
    lane = lax.broadcasted_iota(jnp.int32, block.shape, 1)
    odd = row % 2
    turned = pltpu.roll(block, side, 1)
    above = pltpu.roll(turned, SUB - 1, 0)
    below = pltpu.roll(turned, 1, 0)
    return jnp.where(odd == lane // side, block, jnp.where(odd == 0, above, below))


def flip_rows(block):
    row = lax.broadcasted_iota(jnp.int32, block.shape, 0)
    block = pltpu.roll(block, SUB // 2, 0)
    for step in (2, 1):
        up, down = pltpu.roll(block, SUB - step, 0), pltpu.roll(block, step, 0)
        block = jnp.where((row // step) % 2 == 0, up, down)
    return block


def kernel(
    nf,
    nc,
    rhs_hbm,
    diag_hbm,
    band_hbm,
    reach_hbm,
    tiles_hbm,
    rows_hbm,
    cols_hbm,
    count_hbm,
    sol_ref,
    res_ref,
    rhs_ref,
    diag_ref,
    band_ref,
    reach_ref,
    rows_ref,
    cols_ref,
    count_ref,
    tiles,
    band,
    flipped,
    inv,
    vecs,
    ys,
    row_in,
    col_in,
    halo_in,
    spill_out,
    spill_in,
    row_out,
    col_out,
    row_back,
    col_back,
    last_out,
    last_in,
    pick_row,
    pick_col,
    put_row,
    put_col,
    r_cols,
    c_rows,
    g_cols,
    nus,
    tile_sem,
    load_sem,
    s_row,
    r_row,
    s_col,
    r_col,
    s_halo,
    r_halo,
    s_spill,
    r_spill,
    s_rowb,
    r_rowb,
    s_colb,
    r_colb,
    s_last,
    r_last,
):
    f = lax.axis_index("frames")
    c = lax.axis_index("cols")
    slots, tile, _ = tiles.shape
    side = tile // COMP
    lanes = 2 * side
    chunks = tile // lanes
    blocks = vecs.shape[1]
    frames = blocks * lanes
    slab = blocks * SUB
    reach_len = band_ref.shape[2]

    small = [
        pltpu.make_async_copy(src, dst, load_sem.at[at])
        for at, (src, dst) in enumerate(
            (
                (diag_hbm, diag_ref),
                (rhs_hbm, rhs_ref),
                (rows_hbm, rows_ref),
                (cols_hbm, cols_ref),
                (count_hbm, count_ref),
                (reach_hbm, reach_ref),
                (band_hbm, band_ref),
            )
        )
    ]
    for copy in small:
        copy.start()
    load = pltpu.make_async_copy(tiles_hbm.at[0, 0], tiles, tile_sem)
    load.start()

    row_peers = [(f, lax.rem(c + d, nc)) for d in range(1, nc)]
    col_peers = [(lax.rem(f + d, nf), c) for d in range(1, nf)]
    after = (lax.rem(f + (c + 1) // nc, nf), lax.rem(c + 1, nc))
    before = (lax.rem(f + nf - 1 + (c + nc - 1) // nc, nf), lax.rem(c + nc - 1, nc))
    greet = row_peers + col_peers + [after, before]
    barrier = pltpu.get_barrier_semaphore()
    for peer in greet:
        pl.semaphore_signal(barrier, inc=1, device_id=peer, device_id_type=MESH)

    row_iota = lax.broadcasted_iota(jnp.int32, (SUB, lanes), 0)
    lane_iota = lax.broadcasted_iota(jnp.int32, (SUB, lanes), 1)
    zero = jnp.zeros((SUB, lanes), jnp.float32)

    ys[0] = jnp.zeros((blocks, SUB, lanes), jnp.float32)
    inv[...] = jnp.zeros_like(inv)
    for copy in small:
        copy.wait()
    for h in range(blocks):
        cut = slice(h * lanes, (h + 1) * lanes)
        ys[0, h, 0:COMP, :] = rhs_ref[:, cut]
        for a in range(COMP):
            inv[a, h, 0:COMP, :] = diag_ref[a, :, cut]
    for h in range(blocks):
        mat = [inv[a, h] for a in range(COMP)]
        out = [jnp.where(row_iota == a, 1.0, 0.0) for a in range(COMP)]
        for p in range(COMP):
            pivot = mat[p][p : p + 1, :]
            mat[p] = mat[p] / pivot
            out[p] = out[p] / pivot
            for a in range(COMP):
                if a != p:
                    factor = mat[a][p : p + 1, :]
                    mat[a] = mat[a] - factor * mat[p]
                    out[a] = out[a] - factor * out[p]
        for a in range(COMP):
            inv[a, h] = out[a]

    def precondition(h, value):
        total = zero
        for a in range(COMP):
            total = total + inv[a, h] * value[a : a + 1, :]
        return total

    for h in range(blocks):
        vecs[0, h] = precondition(h, ys[0, h])

    ends = (f == nf - 1) & (c == nc - 1)
    limit = jnp.where(ends, frames, frames + reach_len)
    for h in range(blocks):
        cut = slice(h * lanes, (h + 1) * lanes)
        offset = row_iota + 1
        keep = (offset <= reach_ref[:, cut]) & (lane_iota + h * lanes + offset < limit)
        keep = jnp.where(keep, 1.0, 0.0)
        for a in range(COMP):
            for b in range(COMP):
                block = band_ref[a, b, :, cut] * keep
                band[a, b, h] = block
                flipped[a, b, h] = flip_rows(block)

    count = count_ref[0, 0]

    def targets(ids_ref, iota, width):
        out = jnp.full(iota.shape, -1, jnp.int32)
        slot_at = iota // width
        for s in range(slots):
            at = ids_ref[0, 0, s]
            base = jnp.where(s < count, (at // 2) * SUB + lax.rem(at, 2), -slab * nf * nc)
            for j in range(chunks):
                out = jnp.where(slot_at == j * slots + s, base + 2 * j, out)
        return out

    for ids, pick, put, width in ((rows_ref, pick_row, put_row, 1), (cols_ref, pick_col, put_col, SUB)):
        rows, wide = pick.shape[0], pick.shape[1] // 3
        down = targets(ids, lax.broadcasted_iota(jnp.int32, (rows, 1), 0), 1)
        once = jnp.where(lax.broadcasted_iota(jnp.int32, (rows, wide), 1) == down, 1.0, 0.0)
        pick[...] = jnp.concatenate([once] * 3, axis=1).astype(jnp.bfloat16)
        rows, wide = put.shape[0], put.shape[1] // 3
        along = targets(ids, lax.broadcasted_iota(jnp.int32, (1, wide), 1), width)
        once = jnp.where(lax.broadcasted_iota(jnp.int32, (rows, wide), 0) == along, 1.0, 0.0)
        put[...] = jnp.concatenate([once] * 3, axis=1).astype(jnp.bfloat16)

    pl.semaphore_wait(barrier, len(greet))

    def remote(src, dst, send, recv, peer):
        copy = pltpu.make_async_remote_copy(
            src_ref=src, dst_ref=dst, send_sem=send, recv_sem=recv, device_id=peer, device_id_type=MESH
        )
        copy.start()
        return copy

    def select(pick, value):
        first = value.astype(jnp.bfloat16)
        left = value - first.astype(jnp.float32)
        second = left.astype(jnp.bfloat16)
        third = (left - second.astype(jnp.float32)).astype(jnp.bfloat16)
        parts = jnp.concatenate([first, second, third], axis=0)
        return jnp.dot(pick[...], parts, preferred_element_type=jnp.float32)

    def step(k, carry):
        prev = jnp.maximum(k - 1, 0)
        v = [vecs[k, h] for h in range(blocks)]
        even = jnp.zeros((1, lanes), jnp.float32)
        odd = jnp.zeros((1, lanes), jnp.float32)
        for h in range(blocks):
            y = ys[k, h]
            even = even + jnp.sum(v[h] * y, axis=0, keepdims=True)
            odd = odd + jnp.sum(vecs[prev, h] * y, axis=0, keepdims=True)
        paired = [swap_pairs(v[h], side) for h in range(blocks)]
        paired[0] = jnp.where(row_iota == COMP, even, jnp.where(row_iota == COMP + 1, odd, paired[0]))
        for h in range(blocks):
            row_in[k, c, h * SUB : (h + 1) * SUB, :] = paired[h]
            col_in[k, f, h * SUB : (h + 1) * SUB, :] = paired[h]
        row_gets, col_gets = [], []
        for d in range(1, nf):
            col_gets.append(remote(col_in.at[k, f], col_in.at[k, f], s_col.at[k, d], r_col.at[k, d], col_peers[d - 1]))
        for d in range(1, nc):
            row_gets.append(remote(row_in.at[k, c], row_in.at[k, c], s_row.at[k, d], r_row.at[k, d], row_peers[d - 1]))
        halo = remote(vecs.at[k, 0], halo_in.at[k], s_halo.at[k], r_halo.at[k], before)

        image = [zero] * blocks
        spill = zero
        for b in range(COMP):
            passed = zero
            for h in range(blocks):
                term = zero
                for a in range(COMP):
                    term = term + band[a, b, h] * v[h][a : a + 1, :]
                turned = pltpu.roll(term, 1, 1, stride=1, stride_axis=0)
                moved = jnp.sum(jnp.where(lane_iota > row_iota, turned, passed), axis=0, keepdims=True)
                image[h] = jnp.where(row_iota == b, moved, image[h])
                passed = turned
            moved = jnp.sum(jnp.where(lane_iota > row_iota, 0.0, passed), axis=0, keepdims=True)
            spill = jnp.where(row_iota == b, moved, spill)
        spill_out[k] = spill
        spilled = remote(spill_out.at[k], spill_in.at[k], s_spill.at[k], r_spill.at[k], after)

        for copy in row_gets:
            copy.wait_recv()
        rows_all = row_in[k].reshape(nc * slab, lanes)
        r_cols[...] = select(pick_row, rows_all).T

        @pl.when(k == 0)
        def _():
            load.wait()

        def transposed(i, accs):
            accs = list(accs)
            for u in range(UNROLL):
                at = pl.multiple_of(i * (SUB * UNROLL) + u * SUB, SUB)
                r_now = r_cols[pl.ds(at, SUB), :]
                for s in range(slots):
                    for j in range(chunks):
                        col = j * slots + s
                        spot = pl.multiple_of(j * lanes + at, SUB)
                        x = jnp.broadcast_to(r_now[:, col : col + 1], (SUB, lanes))
                        for n in range(chunks):
                            part = tiles[s, pl.ds(spot, SUB), n * lanes : (n + 1) * lanes]
                            accs[n * slots + s] = accs[n * slots + s] + part * x
            return tuple(accs)

        accs = lax.fori_loop(0, lanes // (SUB * UNROLL), transposed, (zero,) * (slots * chunks))
        col_out[k] = select(put_col, jnp.concatenate(accs, axis=0))
        sums = jnp.zeros((2, lanes), jnp.float32)
        for d in range(nc):
            sums = sums + row_in[k, d, COMP:SUB, :]
        for d in range(nf):
            col_out[k, d * slab + COMP : d * slab + SUB, :] = sums
        backs = []
        for d in range(1, nf):
            peer = col_peers[d - 1]
            part = col_out.at[k, pl.ds(pl.multiple_of(peer[0] * slab, SUB), slab), :]
            backs.append(remote(part, col_back.at[k, f], s_colb.at[k, d], r_colb.at[k, d], peer))
        col_back[k, f] = col_out[k, pl.ds(pl.multiple_of(f * slab, SUB), slab), :]

        halo.wait_recv()
        ext = v + [halo_in[k]]
        forward = [[zero] * COMP for _ in range(blocks)]
        for b in range(COMP):
            turned = [
                pltpu.roll(jnp.broadcast_to(part[b : b + 1, :], (SUB, lanes)), lanes - SUB, 1, stride=1, stride_axis=0)
                for part in ext
            ]
            for h in range(blocks):
                moved = jnp.where(lane_iota - row_iota < lanes - SUB, turned[h], turned[h + 1])
                for a in range(COMP):
                    forward[h][a] = forward[h][a] + flipped[a, b, h] * moved
        quad = jnp.zeros((1, lanes), jnp.float32)
        for h in range(blocks):
            ahead = zero
            for a in range(COMP):
                ahead = jnp.where(row_iota == a, jnp.sum(forward[h][a], axis=0, keepdims=True), ahead)
            quad = quad + jnp.sum(ahead * v[h], axis=0, keepdims=True)
            image[h] = image[h] + ahead

        for copy in col_gets:
            copy.wait_recv()
        cols_all = col_in[k].reshape(nf * slab, lanes)
        c_rows[...] = select(pick_col, cols_all)

        def direct(i, carry):
            for u in range(UNROLL):
                at = pl.multiple_of(i * (SUB * UNROLL) + u * SUB, SUB)
                g_now = zero
                for s in range(slots):
                    for j in range(chunks):
                        spot = pl.multiple_of(j * lanes + at, SUB)
                        dots = None
                        for n in range(chunks):
                            part = tiles[s, pl.ds(spot, SUB), n * lanes : (n + 1) * lanes]
                            here = n * slots + s
                            term = part * c_rows[here : here + 1, :]
                            dots = term if dots is None else dots + term
                        g_now = jnp.where(
                            lane_iota == j * slots + s, jnp.sum(dots, axis=1, keepdims=True), g_now
                        )
                g_cols[pl.ds(at, SUB), :] = g_now
            return carry

        lax.fori_loop(0, lanes // (SUB * UNROLL), direct, 0)
        gains = g_cols[...]
        quad = 2.0 * (quad + jnp.sum(gains * r_cols[...], axis=0, keepdims=True))
        row_out[k] = select(put_row, gains.T)
        for d in range(nc):
            spot = (d + 1) * slab - SUB + COMP
            row_out[k, spot : spot + 1, :] = quad
        for d in range(1, nc):
            peer = row_peers[d - 1]
            part = row_out.at[k, pl.ds(pl.multiple_of(peer[1] * slab, SUB), slab), :]
            backs.append(remote(part, row_back.at[k, c], s_rowb.at[k, d], r_rowb.at[k, d], peer))
        row_back[k, c] = row_out[k, pl.ds(pl.multiple_of(c * slab, SUB), slab), :]
        spilled.wait_recv()
        image[0] = image[0] + spill_in[k]
        for copy in backs:
            copy.wait_recv()
        total = jnp.sum(row_back[k], axis=0) + jnp.sum(col_back[k], axis=0)
        nus[k] = total
        for h in range(blocks):
            part = jnp.where(row_iota < COMP, total[h * SUB : (h + 1) * SUB, :], 0.0)
            image[h] = image[h] + swap_pairs(part, side)
            ys[k + 1, h] = image[h]
            vecs[k + 1, h] = precondition(h, image[h])
        for copy in col_gets + row_gets + [halo, spilled] + backs:
            copy.wait_send()
        return carry

    lax.fori_loop(0, ITERS, step, 0)

    last = ITERS - 1
    last_out[...] = nus[last, slab - SUB : slab, :]
    finals = []
    for d in range(1, nf):
        finals.append(remote(last_out, last_in.at[f], s_last.at[d], r_last.at[d], col_peers[d - 1]))
    last_in[f] = last_out[...]

    moments = []
    for k in range(ITERS):
        if k:
            moments.append(jnp.sum(nus[k, COMP + 1 : COMP + 2, :], axis=1, keepdims=True))
        moments.append(jnp.sum(nus[k, COMP : COMP + 1, :], axis=1, keepdims=True))

    def quadratic(coefs, values):
        sums = {}
        for i, left in enumerate(coefs):
            for j, right in enumerate(coefs):
                sums.setdefault(i + j, []).append(left * right)
        total = None
        for at, terms in sums.items():
            term = sum(terms[1:], terms[0]) * values(at)
            total = term if total is None else total + term
        return total

    one = jnp.ones((1, 1), jnp.float32)
    none = jnp.zeros((1, 1), jnp.float32)
    rho = [one]
    pi = [one]
    xi = []
    gamma = quadratic(rho, lambda at: moments[at])
    for iteration in range(ITERS):
        if iteration == last:
            for copy in finals:
                copy.wait_recv()
            ending = jnp.sum(last_in[...], axis=0)[COMP : COMP + 1, :]
            moments.append(jnp.sum(ending, axis=1, keepdims=True))
        alpha = gamma / quadratic(pi, lambda at: moments[at] + moments[at + 1])
        xi = [x + alpha * p for x, p in zip(xi + [none] * (len(pi) - len(xi)), pi)]
        image = [(pi[i] if i < len(pi) else none) + (pi[i - 1] if i else none) for i in range(len(pi) + 1)]
        rho = [r - alpha * s for r, s in zip(rho + [none], image)]
        if iteration < last:
            fresh = quadratic(rho, lambda at: moments[at])
            beta = fresh / gamma
            pi = [r + beta * p for r, p in zip(rho, pi + [none])]
            gamma = fresh

    for h in range(blocks):
        cut = slice(h * lanes, (h + 1) * lanes)
        sol = zero
        res = zero
        for k in range(ITERS):
            sol = sol + xi[k] * vecs[k, h]
        for k in range(ITERS + 1):
            res = res + rho[k] * ys[k, h]
        sol_ref[:, cut] = sol[0:COMP, :]
        res_ref[:, cut] = res[0:COMP, :]
    for copy in finals:
        copy.wait_send()


def per_device(nf, nc, right_side, diag_blocks, band_blocks, reach, tiles, tile_rows, tile_cols, tile_count):
    slots, tile = tiles.shape[2], tiles.shape[3]
    lanes = 2 * (tile // COMP)
    chunks = tile // lanes
    frames = right_side.shape[1]
    blocks = frames // lanes
    slab = blocks * SUB
    reach_len = band_blocks.shape[0]
    padded = -(-slots * chunks // lanes) * lanes
    f32 = jnp.float32
    vmem = pl.BlockSpec(memory_space=pltpu.VMEM)
    dma = pltpu.SemaphoreType.DMA
    bf16 = jnp.bfloat16
    scratch = [
        pltpu.VMEM(right_side.shape, f32),
        pltpu.VMEM(diag_blocks.shape, f32),
        pltpu.VMEM((COMP, COMP, reach_len, frames), f32),
        pltpu.VMEM((1, frames), jnp.int32),
        pltpu.SMEM(tile_rows.shape, jnp.int32),
        pltpu.SMEM(tile_cols.shape, jnp.int32),
        pltpu.SMEM(tile_count.shape, jnp.int32),
        pltpu.VMEM((slots, tile, tile), f32),
        pltpu.VMEM((COMP, COMP, blocks, SUB, lanes), f32),
        pltpu.VMEM((COMP, COMP, blocks, SUB, lanes), f32),
        pltpu.VMEM((COMP, blocks, SUB, lanes), f32),
        pltpu.VMEM((ITERS + 1, blocks, SUB, lanes), f32),
        pltpu.VMEM((ITERS + 1, blocks, SUB, lanes), f32),
        pltpu.VMEM((ITERS, nc, slab, lanes), f32),
        pltpu.VMEM((ITERS, nf, slab, lanes), f32),
        pltpu.VMEM((ITERS, SUB, lanes), f32),
        pltpu.VMEM((ITERS, SUB, lanes), f32),
        pltpu.VMEM((ITERS, SUB, lanes), f32),
        pltpu.VMEM((ITERS, nc * slab, lanes), f32),
        pltpu.VMEM((ITERS, nf * slab, lanes), f32),
        pltpu.VMEM((ITERS, nc, slab, lanes), f32),
        pltpu.VMEM((ITERS, nf, slab, lanes), f32),
        pltpu.VMEM((SUB, lanes), f32),
        pltpu.VMEM((nf, SUB, lanes), f32),
        pltpu.VMEM((padded, 3 * nc * slab), bf16),
        pltpu.VMEM((padded, 3 * nf * slab), bf16),
        pltpu.VMEM((nc * slab, 3 * padded), bf16),
        pltpu.VMEM((nf * slab, 3 * slots * chunks * SUB), bf16),
        pltpu.VMEM((lanes, padded), f32),
        pltpu.VMEM((padded, lanes), f32),
        pltpu.VMEM((lanes, padded), f32),
        pltpu.VMEM((ITERS, slab, lanes), f32),
        dma,
        dma((7,)),
    ]
    for shape in ((ITERS, nc), (ITERS, nf), (ITERS,), (ITERS,), (ITERS, nc), (ITERS, nf), (nf,)):
        scratch += [dma(shape), dma(shape)]
    return pl.pallas_call(
        functools.partial(kernel, nf, nc),
        out_shape=(jax.ShapeDtypeStruct(right_side.shape, f32), jax.ShapeDtypeStruct(right_side.shape, f32)),
        in_specs=[pl.BlockSpec(memory_space=pltpu.HBM)] * 8,
        out_specs=(vmem, vmem),
        scratch_shapes=scratch,
        compiler_params=pltpu.CompilerParams(
            collective_id=0, has_side_effects=True, vmem_limit_bytes=60 * 1024 * 1024
        ),
        cost_estimate=pl.CostEstimate(
            flops=4 * ITERS * tiles.size, bytes_accessed=4 * (tiles.size + band_blocks.size), transcendentals=0
        ),
    )(right_side, diag_blocks, band_blocks.transpose(1, 2, 0, 3), reach.reshape(1, -1), tiles, tile_rows, tile_cols, tile_count)


def solution(mesh):
    return jax.shard_map(
        functools.partial(per_device, mesh.shape["frames"], mesh.shape["cols"]),
        mesh=mesh,
        in_specs=(
            P(None, ("frames", "cols")),
            P(None, None, ("frames", "cols")),
            P(None, None, None, ("frames", "cols")),
            P(("frames", "cols")),
            P("frames", "cols", None, None, None),
            P("frames", "cols", None),
            P("frames", "cols", None),
            P("frames", "cols"),
        ),
        out_specs=(P(None, ("frames", "cols")), P(None, ("frames", "cols"))),
        check_vma=False,
    )
```

```python
import functools

import jax
import jax.numpy as jnp
from jax import lax
from jax.experimental import pallas as pl
from jax.experimental.pallas import tpu as pltpu
from jax.sharding import PartitionSpec as P

ITERS = 4
COMP = 6
SUB = 8
UNROLL = 4
MESH = pl.DeviceIdType.MESH


def swap_pairs(block, side):
    row = lax.broadcasted_iota(jnp.int32, block.shape, 0)
    lane = lax.broadcasted_iota(jnp.int32, block.shape, 1)
    odd = row % 2
    turned = pltpu.roll(block, side, 1)
    above = pltpu.roll(turned, SUB - 1, 0)
    below = pltpu.roll(turned, 1, 0)
    return jnp.where(odd == lane // side, block, jnp.where(odd == 0, above, below))


def flip_rows(block):
    row = lax.broadcasted_iota(jnp.int32, block.shape, 0)
    block = pltpu.roll(block, SUB // 2, 0)
    for step in (2, 1):
        up, down = pltpu.roll(block, SUB - step, 0), pltpu.roll(block, step, 0)
        block = jnp.where((row // step) % 2 == 0, up, down)
    return block


def kernel(
    nf,
    nc,
    rhs_hbm,
    diag_hbm,
    band_hbm,
    reach_hbm,
    tiles_hbm,
    rows_hbm,
    cols_hbm,
    count_hbm,
    out_ref,
    rhs_ref,
    diag_ref,
    band_ref,
    reach_ref,
    rows_ref,
    cols_ref,
    count_ref,
    tiles,
    band,
    flipped,
    inv,
    vecs,
    ys,
    row_in,
    col_in,
    halo_in,
    spill_out,
    spill_in,
    row_out,
    col_out,
    row_back,
    col_back,
    quad_out,
    quad_in,
    last_out,
    last_in,
    pick_row,
    pick_col,
    put_row,
    put_col,
    r_cols,
    c_rows,
    g_cols,
    col_acc,
    nus,
    tile_sem,
    load_sem,
    s_row,
    r_row,
    s_col,
    r_col,
    s_halo,
    r_halo,
    s_spill,
    r_spill,
    s_rowb,
    r_rowb,
    s_colb,
    r_colb,
    s_quad,
    r_quad,
    s_last,
    r_last,
):
    f = lax.axis_index("frames")
    c = lax.axis_index("cols")
    slots, tile, _ = tiles.shape
    side = tile // COMP
    lanes = 2 * side
    chunks = tile // lanes
    blocks = vecs.shape[1]
    frames = blocks * lanes
    slab = blocks * SUB
    reach_len = band_ref.shape[2]

    small = [
        pltpu.make_async_copy(src, dst, load_sem.at[at])
        for at, (src, dst) in enumerate(
            (
                (diag_hbm, diag_ref),
                (rhs_hbm, rhs_ref),
                (rows_hbm, rows_ref),
                (cols_hbm, cols_ref),
                (count_hbm, count_ref),
                (reach_hbm, reach_ref),
                (band_hbm, band_ref),
            )
        )
    ]
    for copy in small:
        copy.start()
    loads = [pltpu.make_async_copy(tiles_hbm.at[0, 0, t], tiles.at[t], tile_sem.at[t]) for t in range(slots)]
    for copy in loads:
        copy.start()

    row_peers = [(f, lax.rem(c + d, nc)) for d in range(1, nc)]
    col_peers = [(lax.rem(f + d, nf), c) for d in range(1, nf)]
    after = (lax.rem(f + (c + 1) // nc, nf), lax.rem(c + 1, nc))
    before = (lax.rem(f + nf - 1 + (c + nc - 1) // nc, nf), lax.rem(c + nc - 1, nc))
    greet = row_peers + col_peers + [after, before]
    barrier = pltpu.get_barrier_semaphore()
    for peer in greet:
        pl.semaphore_signal(barrier, inc=1, device_id=peer, device_id_type=MESH)

    row_iota = lax.broadcasted_iota(jnp.int32, (SUB, lanes), 0)
    lane_iota = lax.broadcasted_iota(jnp.int32, (SUB, lanes), 1)
    zero = jnp.zeros((SUB, lanes), jnp.float32)

    ys[0] = jnp.zeros((blocks, SUB, lanes), jnp.float32)
    inv[...] = jnp.zeros_like(inv)
    for copy in small[:2]:
        copy.wait()
    for h in range(blocks):
        cut = slice(h * lanes, (h + 1) * lanes)
        ys[0, h, 0:COMP, :] = rhs_ref[:, cut]
        for a in range(COMP):
            inv[a, h, 0:COMP, :] = diag_ref[a, :, cut]
    for h in range(blocks):
        mat = [inv[a, h] for a in range(COMP)]
        out = [jnp.where(row_iota == a, 1.0, 0.0) for a in range(COMP)]
        for p in range(COMP):
            pivot = mat[p][p : p + 1, :]
            mat[p] = mat[p] / pivot
            out[p] = out[p] / pivot
            for a in range(COMP):
                if a != p:
                    factor = mat[a][p : p + 1, :]
                    mat[a] = mat[a] - factor * mat[p]
                    out[a] = out[a] - factor * out[p]
        for a in range(COMP):
            inv[a, h] = out[a]

    def precondition(h, value):
        total = zero
        for a in range(COMP):
            total = total + inv[a, h] * value[a : a + 1, :]
        return total

    for h in range(blocks):
        vecs[0, h] = precondition(h, ys[0, h])

    pl.semaphore_wait(barrier, len(greet))

    def remote(src, dst, send, recv, peer):
        return pltpu.make_async_remote_copy(
            src_ref=src, dst_ref=dst, send_sem=send, recv_sem=recv, device_id=peer, device_id_type=MESH
        )

    def row_gathers(k):
        return [
            remote(row_in.at[k, c], row_in.at[k, c], s_row.at[k, d], r_row.at[k, d], row_peers[d - 1])
            for d in range(1, nc)
        ]

    def col_gathers(k):
        return [
            remote(col_in.at[k, f], col_in.at[k, f], s_col.at[k, d], r_col.at[k, d], col_peers[d - 1])
            for d in range(1, nf)
        ]

    def halo_copy(k):
        return remote(vecs.at[k, 0], halo_in.at[k], s_halo.at[k], r_halo.at[k], before)

    def spill_copy(k):
        return remote(spill_out.at[k], spill_in.at[k], s_spill.at[k], r_spill.at[k], after)

    def col_returns(k):
        copies = []
        for d in range(1, nf):
            peer = col_peers[d - 1]
            part = col_out.at[k, pl.ds(pl.multiple_of(peer[0] * slab, SUB), slab), :]
            copies.append(remote(part, col_back.at[k, f], s_colb.at[k, d], r_colb.at[k, d], peer))
        return copies

    def row_returns(k):
        copies = []
        for d in range(1, nc):
            peer = row_peers[d - 1]
            part = row_out.at[k, pl.ds(pl.multiple_of(peer[1] * slab, SUB), slab), :]
            copies.append(remote(part, row_back.at[k, c], s_rowb.at[k, d], r_rowb.at[k, d], peer))
        return copies

    def quad_copies():
        return [remote(quad_out, quad_in.at[c], s_quad.at[d], r_quad.at[d], row_peers[d - 1]) for d in range(1, nc)]

    def last_copies():
        return [remote(last_out, last_in.at[f], s_last.at[d], r_last.at[d], col_peers[d - 1]) for d in range(1, nf)]

    def sent(k):
        for copy in row_gathers(k) + col_gathers(k) + [halo_copy(k), spill_copy(k)] + col_returns(k) + row_returns(k):
            copy.wait_send()

    def publish(k):
        prev = jnp.maximum(k - 1, 0)
        even = jnp.zeros((1, lanes), jnp.float32)
        odd = jnp.zeros((1, lanes), jnp.float32)
        for h in range(blocks):
            y = ys[k, h]
            even = even + jnp.sum(vecs[k, h] * y, axis=0, keepdims=True)
            odd = odd + jnp.sum(vecs[prev, h] * y, axis=0, keepdims=True)
        paired = [swap_pairs(vecs[k, h], side) for h in range(blocks)]
        paired[0] = jnp.where(row_iota == COMP, even, jnp.where(row_iota == COMP + 1, odd, paired[0]))
        for h in range(blocks):
            row_in[k, c, h * SUB : (h + 1) * SUB, :] = paired[h]
            col_in[k, f, h * SUB : (h + 1) * SUB, :] = paired[h]
        for copy in row_gathers(k) + col_gathers(k) + [halo_copy(k)]:
            copy.start()

    publish(0)

    for copy in small[2:]:
        copy.wait()

    ends = (f == nf - 1) & (c == nc - 1)
    limit = jnp.where(ends, frames, frames + reach_len)
    for h in range(blocks):
        cut = slice(h * lanes, (h + 1) * lanes)
        offset = row_iota + 1
        keep = (offset <= reach_ref[:, cut]) & (lane_iota + h * lanes + offset < limit)
        keep = jnp.where(keep, 1.0, 0.0)
        for a in range(COMP):
            for b in range(COMP):
                block = band_ref[a, b, :, cut] * keep
                band[a, b, h] = block
                flipped[a, b, h] = flip_rows(block)

    count = count_ref[0, 0]

    def targets(ids_ref, iota, width):
        out = jnp.full(iota.shape, -1, jnp.int32)
        slot_at = iota // width
        for s in range(slots):
            at = ids_ref[0, 0, s]
            base = jnp.where(s < count, (at // 2) * SUB + lax.rem(at, 2), -slab * nf * nc)
            for j in range(chunks):
                out = jnp.where(slot_at == j * slots + s, base + 2 * j, out)
        return out

    for ids, pick, put, width in ((rows_ref, pick_row, put_row, 1), (cols_ref, pick_col, put_col, SUB)):
        rows, wide = pick.shape[0], pick.shape[1] // 3
        down = targets(ids, lax.broadcasted_iota(jnp.int32, (rows, 1), 0), 1)
        once = jnp.where(lax.broadcasted_iota(jnp.int32, (rows, wide), 1) == down, 1.0, 0.0)
        pick[...] = jnp.concatenate([once] * 3, axis=1).astype(jnp.bfloat16)
        rows, wide = put.shape[0], put.shape[1] // 3
        along = targets(ids, lax.broadcasted_iota(jnp.int32, (1, wide), 1), width)
        once = jnp.where(lax.broadcasted_iota(jnp.int32, (rows, wide), 0) == along, 1.0, 0.0)
        put[...] = jnp.concatenate([once] * 3, axis=1).astype(jnp.bfloat16)

    def select(pick, value):
        first = value.astype(jnp.bfloat16)
        left = value - first.astype(jnp.float32)
        second = left.astype(jnp.bfloat16)
        third = (left - second.astype(jnp.float32)).astype(jnp.bfloat16)
        parts = jnp.concatenate([first, second, third], axis=0)
        return jnp.dot(pick[...], parts, preferred_element_type=jnp.float32)

    def step(k, carry):
        v = [vecs[k, h] for h in range(blocks)]

        @pl.when(k > 0)
        def _():
            sent(k - 1)

        image = [zero] * blocks
        spill = zero
        for b in range(COMP):
            passed = zero
            for h in range(blocks):
                term = zero
                for a in range(COMP):
                    term = term + band[a, b, h] * v[h][a : a + 1, :]
                turned = pltpu.roll(term, 1, 1, stride=1, stride_axis=0)
                moved = jnp.sum(jnp.where(lane_iota > row_iota, turned, passed), axis=0, keepdims=True)
                image[h] = jnp.where(row_iota == b, moved, image[h])
                passed = turned
            moved = jnp.sum(jnp.where(lane_iota > row_iota, 0.0, passed), axis=0, keepdims=True)
            spill = jnp.where(row_iota == b, moved, spill)
        spill_out[k] = spill
        spill_copy(k).start()

        for copy in row_gathers(k):
            copy.wait_recv()
        rows_all = row_in[k].reshape(nc * slab, lanes)
        r_cols[...] = select(pick_row, rows_all).T

        @pl.when(k == 0)
        def _():
            for copy in loads:
                copy.wait()

        def transposed(i, accs):
            accs = list(accs)
            for u in range(UNROLL):
                at = pl.multiple_of(i * (SUB * UNROLL) + u * SUB, SUB)
                r_now = r_cols[pl.ds(at, SUB), :]
                for s in range(slots):
                    for j in range(chunks):
                        col = j * slots + s
                        spot = pl.multiple_of(j * lanes + at, SUB)
                        x = jnp.broadcast_to(r_now[:, col : col + 1], (SUB, lanes))
                        for n in range(chunks):
                            part = tiles[s, pl.ds(spot, SUB), n * lanes : (n + 1) * lanes]
                            accs[n * slots + s] = accs[n * slots + s] + part * x
            return tuple(accs)

        accs = lax.fori_loop(0, lanes // (SUB * UNROLL), transposed, (zero,) * (slots * chunks))
        for q, acc in enumerate(accs):
            col_acc[q * SUB : (q + 1) * SUB, :] = acc
        col_out[k] = select(put_col, col_acc[...])
        sums = jnp.zeros((2, lanes), jnp.float32)
        for d in range(nc):
            sums = sums + row_in[k, d, COMP:SUB, :]
        for d in range(nf):
            col_out[k, d * slab + COMP : d * slab + SUB, :] = sums
        for copy in col_returns(k):
            copy.start()
        col_back[k, f] = col_out[k, pl.ds(pl.multiple_of(f * slab, SUB), slab), :]

        halo_copy(k).wait_recv()
        ext = v + [halo_in[k]]
        forward = [[zero] * COMP for _ in range(blocks)]
        for b in range(COMP):
            turned = [
                pltpu.roll(jnp.broadcast_to(part[b : b + 1, :], (SUB, lanes)), lanes - SUB, 1, stride=1, stride_axis=0)
                for part in ext
            ]
            for h in range(blocks):
                moved = jnp.where(lane_iota - row_iota < lanes - SUB, turned[h], turned[h + 1])
                for a in range(COMP):
                    forward[h][a] = forward[h][a] + flipped[a, b, h] * moved
        quad = jnp.zeros((1, lanes), jnp.float32)
        for h in range(blocks):
            ahead = zero
            for a in range(COMP):
                ahead = jnp.where(row_iota == a, jnp.sum(forward[h][a], axis=0, keepdims=True), ahead)
            quad = quad + jnp.sum(ahead * v[h], axis=0, keepdims=True)
            image[h] = image[h] + ahead

        for copy in col_gathers(k):
            copy.wait_recv()
        cols_all = col_in[k].reshape(nf * slab, lanes)
        c_rows[...] = select(pick_col, cols_all)

        @pl.when(k == last)
        def _():
            both = zero
            for q in range(slots * chunks):
                both = both + col_acc[q * SUB : (q + 1) * SUB, :] * c_rows[q : q + 1, :]
            part = 2.0 * (quad + jnp.sum(both, axis=0, keepdims=True))
            quad_out[...] = jnp.broadcast_to(part, (SUB, lanes))
            for copy in quad_copies():
                copy.start()
            quad_in[c] = quad_out[...]

        def direct(i, carry):
            for u in range(UNROLL):
                at = pl.multiple_of(i * (SUB * UNROLL) + u * SUB, SUB)
                g_now = zero
                for s in range(slots):
                    for j in range(chunks):
                        spot = pl.multiple_of(j * lanes + at, SUB)
                        dots = None
                        for n in range(chunks):
                            part = tiles[s, pl.ds(spot, SUB), n * lanes : (n + 1) * lanes]
                            here = n * slots + s
                            term = part * c_rows[here : here + 1, :]
                            dots = term if dots is None else dots + term
                        g_now = jnp.where(
                            lane_iota == j * slots + s, jnp.sum(dots, axis=1, keepdims=True), g_now
                        )
                g_cols[pl.ds(at, SUB), :] = g_now
            return carry

        lax.fori_loop(0, lanes // (SUB * UNROLL), direct, 0)

        @pl.when(k == last)
        def _():
            for copy in quad_copies():
                copy.wait_recv()
            last_out[...] = jnp.sum(quad_in[...], axis=0)
            for copy in last_copies():
                copy.start()
            last_in[f] = last_out[...]

        row_out[k] = select(put_row, g_cols[...].T)
        for copy in row_returns(k):
            copy.start()
        row_back[k, c] = row_out[k, pl.ds(pl.multiple_of(c * slab, SUB), slab), :]
        spill_copy(k).wait_recv()
        image[0] = image[0] + spill_in[k]
        for copy in col_returns(k) + row_returns(k):
            copy.wait_recv()
        total = jnp.sum(row_back[k], axis=0) + jnp.sum(col_back[k], axis=0)
        nus[k] = total[0:SUB, :]
        for h in range(blocks):
            part = jnp.where(row_iota < COMP, total[h * SUB : (h + 1) * SUB, :], 0.0)
            image[h] = image[h] + swap_pairs(part, side)
            ys[k + 1, h] = image[h]

        @pl.when(k < last)
        def _():
            for h in range(blocks):
                vecs[k + 1, h] = precondition(h, image[h])
            publish(k + 1)

        return carry

    last = ITERS - 1
    lax.fori_loop(0, ITERS, step, 0)

    moments = []
    for k in range(ITERS):
        if k:
            moments.append(jnp.sum(nus[k, COMP + 1 : COMP + 2, :], axis=1, keepdims=True))
        moments.append(jnp.sum(nus[k, COMP : COMP + 1, :], axis=1, keepdims=True))

    def quadratic(coefs, values):
        sums = {}
        for i, left in enumerate(coefs):
            for j, right in enumerate(coefs):
                sums.setdefault(i + j, []).append(left * right)
        total = None
        for at, terms in sums.items():
            term = sum(terms[1:], terms[0]) * values(at)
            total = term if total is None else total + term
        return total

    one = jnp.ones((1, 1), jnp.float32)
    none = jnp.zeros((1, 1), jnp.float32)
    rho = [one]
    pi = [one]
    xi = []
    gamma = quadratic(rho, lambda at: moments[at])
    for iteration in range(ITERS):
        if iteration == last:
            for copy in last_copies():
                copy.wait_recv()
            ending = jnp.sum(last_in[...], axis=0)[0:1, :]
            moments.append(jnp.sum(ending, axis=1, keepdims=True))
        alpha = gamma / quadratic(pi, lambda at: moments[at] + moments[at + 1])
        xi = [x + alpha * p for x, p in zip(xi + [none] * (len(pi) - len(xi)), pi)]
        image = [(pi[i] if i < len(pi) else none) + (pi[i - 1] if i else none) for i in range(len(pi) + 1)]
        rho = [r - alpha * s for r, s in zip(rho + [none], image)]
        if iteration < last:
            fresh = quadratic(rho, lambda at: moments[at])
            beta = fresh / gamma
            pi = [r + beta * p for r, p in zip(rho, pi + [none])]
            gamma = fresh

    for h in range(blocks):
        cut = slice(h * lanes, (h + 1) * lanes)
        sol = zero
        res = zero
        for k in range(ITERS):
            sol = sol + xi[k] * vecs[k, h]
        for k in range(ITERS + 1):
            res = res + rho[k] * ys[k, h]
        out_ref[0, :, cut] = sol[0:COMP, :]
        out_ref[1, :, cut] = res[0:COMP, :]
    sent(last)
    for copy in quad_copies() + last_copies():
        copy.wait_send()


def per_device(nf, nc, right_side, diag_blocks, band_blocks, reach, tiles, tile_rows, tile_cols, tile_count):
    slots, tile = tiles.shape[2], tiles.shape[3]
    lanes = 2 * (tile // COMP)
    chunks = tile // lanes
    frames = right_side.shape[1]
    blocks = frames // lanes
    slab = blocks * SUB
    reach_len = band_blocks.shape[0]
    padded = -(-slots * chunks // lanes) * lanes
    f32 = jnp.float32
    vmem = pl.BlockSpec(memory_space=pltpu.VMEM)
    dma = pltpu.SemaphoreType.DMA
    bf16 = jnp.bfloat16
    scratch = [
        pltpu.VMEM(right_side.shape, f32),
        pltpu.VMEM(diag_blocks.shape, f32),
        pltpu.VMEM((COMP, COMP, reach_len, frames), f32),
        pltpu.VMEM((1, frames), jnp.int32),
        pltpu.SMEM(tile_rows.shape, jnp.int32),
        pltpu.SMEM(tile_cols.shape, jnp.int32),
        pltpu.SMEM(tile_count.shape, jnp.int32),
        pltpu.VMEM((slots, tile, tile), f32),
        pltpu.VMEM((COMP, COMP, blocks, SUB, lanes), f32),
        pltpu.VMEM((COMP, COMP, blocks, SUB, lanes), f32),
        pltpu.VMEM((COMP, blocks, SUB, lanes), f32),
        pltpu.VMEM((ITERS + 1, blocks, SUB, lanes), f32),
        pltpu.VMEM((ITERS + 1, blocks, SUB, lanes), f32),
        pltpu.VMEM((ITERS, nc, slab, lanes), f32),
        pltpu.VMEM((ITERS, nf, slab, lanes), f32),
        pltpu.VMEM((ITERS, SUB, lanes), f32),
        pltpu.VMEM((ITERS, SUB, lanes), f32),
        pltpu.VMEM((ITERS, SUB, lanes), f32),
        pltpu.VMEM((ITERS, nc * slab, lanes), f32),
        pltpu.VMEM((ITERS, nf * slab, lanes), f32),
        pltpu.VMEM((ITERS, nc, slab, lanes), f32),
        pltpu.VMEM((ITERS, nf, slab, lanes), f32),
        pltpu.VMEM((SUB, lanes), f32),
        pltpu.VMEM((nc, SUB, lanes), f32),
        pltpu.VMEM((SUB, lanes), f32),
        pltpu.VMEM((nf, SUB, lanes), f32),
        pltpu.VMEM((padded, 3 * nc * slab), bf16),
        pltpu.VMEM((padded, 3 * nf * slab), bf16),
        pltpu.VMEM((nc * slab, 3 * padded), bf16),
        pltpu.VMEM((nf * slab, 3 * slots * chunks * SUB), bf16),
        pltpu.VMEM((lanes, padded), f32),
        pltpu.VMEM((padded, lanes), f32),
        pltpu.VMEM((lanes, padded), f32),
        pltpu.VMEM((slots * chunks * SUB, lanes), f32),
        pltpu.VMEM((ITERS, SUB, lanes), f32),
        dma((slots,)),
        dma((7,)),
    ]
    for shape in ((ITERS, nc), (ITERS, nf), (ITERS,), (ITERS,), (ITERS, nc), (ITERS, nf), (nc,), (nf,)):
        scratch += [dma(shape), dma(shape)]
    out = pl.pallas_call(
        functools.partial(kernel, nf, nc),
        out_shape=jax.ShapeDtypeStruct((2,) + right_side.shape, f32),
        in_specs=[pl.BlockSpec(memory_space=pltpu.HBM)] * 8,
        out_specs=vmem,
        scratch_shapes=scratch,
        compiler_params=pltpu.CompilerParams(
            collective_id=0, has_side_effects=True, vmem_limit_bytes=60 * 1024 * 1024
        ),
        cost_estimate=pl.CostEstimate(
            flops=4 * ITERS * tiles.size, bytes_accessed=4 * (tiles.size + band_blocks.size), transcendentals=0
        ),
    )(right_side, diag_blocks, band_blocks.transpose(1, 2, 0, 3), reach.reshape(1, -1), tiles, tile_rows, tile_cols, tile_count)
    return out[0], out[1]


def solution(mesh):
    return jax.shard_map(
        functools.partial(per_device, mesh.shape["frames"], mesh.shape["cols"]),
        mesh=mesh,
        in_specs=(
            P(None, ("frames", "cols")),
            P(None, None, ("frames", "cols")),
            P(None, None, None, ("frames", "cols")),
            P(("frames", "cols")),
            P("frames", "cols", None, None, None),
            P("frames", "cols", None),
            P("frames", "cols", None),
            P("frames", "cols"),
        ),
        out_specs=(P(None, ("frames", "cols")), P(None, ("frames", "cols"))),
        check_vma=False,
    )
```

```python
import functools

import jax
import jax.numpy as jnp
from jax import lax
from jax.experimental import pallas as pl
from jax.experimental.pallas import tpu as pltpu
from jax.sharding import PartitionSpec as P

ITERS = 4
COMP = 6
SUB = 8
PART = 32
MESH = pl.DeviceIdType.MESH


def swap_pairs(block, side):
    row = lax.broadcasted_iota(jnp.int32, block.shape, 0)
    lane = lax.broadcasted_iota(jnp.int32, block.shape, 1)
    odd = row % 2
    turned = pltpu.roll(block, side, 1)
    above = pltpu.roll(turned, SUB - 1, 0)
    below = pltpu.roll(turned, 1, 0)
    return jnp.where(odd == lane // side, block, jnp.where(odd == 0, above, below))


def flip_rows(block):
    row = lax.broadcasted_iota(jnp.int32, block.shape, 0)
    block = pltpu.roll(block, SUB // 2, 0)
    for step in (2, 1):
        up, down = pltpu.roll(block, SUB - step, 0), pltpu.roll(block, step, 0)
        block = jnp.where((row // step) % 2 == 0, up, down)
    return block


def kernel(
    nf,
    nc,
    rhs_hbm,
    diag_hbm,
    band_hbm,
    reach_hbm,
    tiles_hbm,
    rows_hbm,
    cols_hbm,
    count_hbm,
    out_ref,
    rhs_ref,
    diag_ref,
    band_ref,
    reach_ref,
    rows_ref,
    cols_ref,
    count_ref,
    tiles,
    high,
    low,
    band,
    flipped,
    inv,
    vecs,
    ys,
    row_in,
    col_in,
    halo_in,
    spill_out,
    spill_in,
    row_out,
    col_out,
    row_back,
    col_back,
    quad_out,
    quad_in,
    last_out,
    last_in,
    pick_row,
    pick_col,
    put_row,
    put_col,
    col_acc,
    nus,
    tile_sem,
    load_sem,
    s_row,
    r_row,
    s_col,
    r_col,
    s_halo,
    r_halo,
    s_spill,
    r_spill,
    s_rowb,
    r_rowb,
    s_colb,
    r_colb,
    s_quad,
    r_quad,
    s_last,
    r_last,
):
    f = lax.axis_index("frames")
    c = lax.axis_index("cols")
    slots, tile, _ = tiles.shape
    side = tile // COMP
    lanes = 2 * side
    chunks = tile // lanes
    blocks = vecs.shape[1]
    frames = blocks * lanes
    slab = blocks * SUB
    reach_len = band_ref.shape[2]

    small = [
        pltpu.make_async_copy(src, dst, load_sem.at[at])
        for at, (src, dst) in enumerate(
            (
                (diag_hbm, diag_ref),
                (rhs_hbm, rhs_ref),
                (rows_hbm, rows_ref),
                (cols_hbm, cols_ref),
                (count_hbm, count_ref),
                (reach_hbm, reach_ref),
                (band_hbm, band_ref),
            )
        )
    ]
    for copy in small:
        copy.start()
    loads = [pltpu.make_async_copy(tiles_hbm.at[0, 0, t], tiles.at[t], tile_sem.at[t]) for t in range(slots)]
    for copy in loads:
        copy.start()

    row_peers = [(f, lax.rem(c + d, nc)) for d in range(1, nc)]
    col_peers = [(lax.rem(f + d, nf), c) for d in range(1, nf)]
    after = (lax.rem(f + (c + 1) // nc, nf), lax.rem(c + 1, nc))
    before = (lax.rem(f + nf - 1 + (c + nc - 1) // nc, nf), lax.rem(c + nc - 1, nc))
    greet = row_peers + col_peers + [after, before]
    barrier = pltpu.get_barrier_semaphore()
    for peer in greet:
        pl.semaphore_signal(barrier, inc=1, device_id=peer, device_id_type=MESH)

    row_iota = lax.broadcasted_iota(jnp.int32, (SUB, lanes), 0)
    lane_iota = lax.broadcasted_iota(jnp.int32, (SUB, lanes), 1)
    zero = jnp.zeros((SUB, lanes), jnp.float32)

    ys[0] = jnp.zeros((blocks, SUB, lanes), jnp.float32)
    inv[...] = jnp.zeros_like(inv)
    for copy in small[:2]:
        copy.wait()
    for h in range(blocks):
        cut = slice(h * lanes, (h + 1) * lanes)
        ys[0, h, 0:COMP, :] = rhs_ref[:, cut]
        for a in range(COMP):
            inv[a, h, 0:COMP, :] = diag_ref[a, :, cut]
    for h in range(blocks):
        mat = [inv[a, h] for a in range(COMP)]
        out = [jnp.where(row_iota == a, 1.0, 0.0) for a in range(COMP)]
        for p in range(COMP):
            pivot = mat[p][p : p + 1, :]
            mat[p] = mat[p] / pivot
            out[p] = out[p] / pivot
            for a in range(COMP):
                if a != p:
                    factor = mat[a][p : p + 1, :]
                    mat[a] = mat[a] - factor * mat[p]
                    out[a] = out[a] - factor * out[p]
        for a in range(COMP):
            inv[a, h] = out[a]

    def precondition(h, value):
        total = zero
        for a in range(COMP):
            total = total + inv[a, h] * value[a : a + 1, :]
        return total

    for h in range(blocks):
        vecs[0, h] = precondition(h, ys[0, h])

    pl.semaphore_wait(barrier, len(greet))

    def remote(src, dst, send, recv, peer):
        return pltpu.make_async_remote_copy(
            src_ref=src, dst_ref=dst, send_sem=send, recv_sem=recv, device_id=peer, device_id_type=MESH
        )

    def row_gathers(k):
        return [
            remote(row_in.at[k, c], row_in.at[k, c], s_row.at[k, d], r_row.at[k, d], row_peers[d - 1])
            for d in range(1, nc)
        ]

    def col_gathers(k):
        return [
            remote(col_in.at[k, f], col_in.at[k, f], s_col.at[k, d], r_col.at[k, d], col_peers[d - 1])
            for d in range(1, nf)
        ]

    def halo_copy(k):
        return remote(vecs.at[k, 0], halo_in.at[k], s_halo.at[k], r_halo.at[k], before)

    def spill_copy(k):
        return remote(spill_out.at[k], spill_in.at[k], s_spill.at[k], r_spill.at[k], after)

    def col_returns(k):
        copies = []
        for d in range(1, nf):
            peer = col_peers[d - 1]
            part = col_out.at[k, pl.ds(pl.multiple_of(peer[0] * slab, SUB), slab), :]
            copies.append(remote(part, col_back.at[k, f], s_colb.at[k, d], r_colb.at[k, d], peer))
        return copies

    def row_returns(k):
        copies = []
        for d in range(1, nc):
            peer = row_peers[d - 1]
            part = row_out.at[k, pl.ds(pl.multiple_of(peer[1] * slab, SUB), slab), :]
            copies.append(remote(part, row_back.at[k, c], s_rowb.at[k, d], r_rowb.at[k, d], peer))
        return copies

    def quad_copies():
        return [remote(quad_out, quad_in.at[c], s_quad.at[d], r_quad.at[d], row_peers[d - 1]) for d in range(1, nc)]

    def last_copies():
        return [remote(last_out, last_in.at[f], s_last.at[d], r_last.at[d], col_peers[d - 1]) for d in range(1, nf)]

    def sent(k):
        for copy in row_gathers(k) + col_gathers(k) + [halo_copy(k), spill_copy(k)] + col_returns(k) + row_returns(k):
            copy.wait_send()

    def publish(k):
        prev = jnp.maximum(k - 1, 0)
        even = jnp.zeros((1, lanes), jnp.float32)
        odd = jnp.zeros((1, lanes), jnp.float32)
        for h in range(blocks):
            y = ys[k, h]
            even = even + jnp.sum(vecs[k, h] * y, axis=0, keepdims=True)
            odd = odd + jnp.sum(vecs[prev, h] * y, axis=0, keepdims=True)
        paired = [swap_pairs(vecs[k, h], side) for h in range(blocks)]
        paired[0] = jnp.where(row_iota == COMP, even, jnp.where(row_iota == COMP + 1, odd, paired[0]))
        for h in range(blocks):
            row_in[k, c, h * SUB : (h + 1) * SUB, :] = paired[h]
            col_in[k, f, h * SUB : (h + 1) * SUB, :] = paired[h]
        for copy in row_gathers(k) + col_gathers(k) + [halo_copy(k)]:
            copy.start()

    publish(0)

    for copy in small[2:]:
        copy.wait()

    ends = (f == nf - 1) & (c == nc - 1)
    limit = jnp.where(ends, frames, frames + reach_len)
    for h in range(blocks):
        cut = slice(h * lanes, (h + 1) * lanes)
        offset = row_iota + 1
        keep = (offset <= reach_ref[:, cut]) & (lane_iota + h * lanes + offset < limit)
        keep = jnp.where(keep, 1.0, 0.0)
        for a in range(COMP):
            for b in range(COMP):
                block = band_ref[a, b, :, cut] * keep
                band[a, b, h] = block
                flipped[a, b, h] = flip_rows(block)

    count = count_ref[0, 0]

    def targets(ids_ref, iota):
        out = jnp.full(iota.shape, -1, jnp.int32)
        for s in range(slots):
            at = ids_ref[0, 0, s]
            base = jnp.where(s < count, (at // 2) * SUB + lax.rem(at, 2), -slab * nf * nc)
            for j in range(chunks):
                out = jnp.where(iota == j * slots + s, base + 2 * j, out)
        return out

    for ids, pick, put in ((rows_ref, pick_row, put_row), (cols_ref, pick_col, put_col)):
        rows, wide = pick.shape[0], pick.shape[1] // 3
        down = targets(ids, lax.broadcasted_iota(jnp.int32, (rows, 1), 0))
        once = jnp.where(lax.broadcasted_iota(jnp.int32, (rows, wide), 1) == down, 1.0, 0.0)
        pick[...] = jnp.concatenate([once] * 3, axis=1).astype(jnp.bfloat16)
        rows, wide = put.shape[0], put.shape[1] // 3
        along = targets(ids, lax.broadcasted_iota(jnp.int32, (1, wide), 1))
        once = jnp.where(lax.broadcasted_iota(jnp.int32, (rows, wide), 0) == along, 1.0, 0.0)
        put[...] = jnp.concatenate([once] * 3, axis=1).astype(jnp.bfloat16)

    def select(pick, value):
        first = value.astype(jnp.bfloat16)
        left = value - first.astype(jnp.float32)
        second = left.astype(jnp.bfloat16)
        third = (left - second.astype(jnp.float32)).astype(jnp.bfloat16)
        parts = jnp.concatenate([first, second, third], axis=0)
        return jnp.dot(pick[...], parts, preferred_element_type=jnp.float32)

    tile_row = lax.broadcasted_iota(jnp.int32, (slots, tile), 0)
    many = slots * chunks

    def products(rows, contract):
        value = jnp.concatenate([rows[j * slots : (j + 1) * slots, :] for j in range(chunks)], axis=1)
        first = value.astype(jnp.bfloat16).astype(jnp.float32)
        second = (value - first).astype(jnp.bfloat16).astype(jnp.float32)
        third = value - first - second
        left = jnp.concatenate([first, second, third, jnp.zeros_like(third)], axis=0).astype(jnp.bfloat16)
        out = jnp.zeros((slots, tile), jnp.float32)
        for s in range(slots):
            full = None
            for part in (high, low):
                term = lax.dot_general(
                    left, part[s], (((1,), (contract,)), ((), ())), preferred_element_type=jnp.float32
                )
                full = term if full is None else full + term
            kept = full[:slots] + full[slots : 2 * slots] + full[2 * slots : 3 * slots]
            out = jnp.where(tile_row == s, kept, out)
        pieces = [out[:, j * lanes : (j + 1) * lanes] for j in range(chunks)]
        if rows.shape[0] > many:
            pieces.append(jnp.zeros((rows.shape[0] - many, lanes), jnp.float32))
        return jnp.concatenate(pieces, axis=0)

    for s in range(slots):
        loads[s].wait()

        def split(i, carry, s=s):
            spot = pl.ds(pl.multiple_of(i * PART, PART), PART)
            whole = tiles[s, spot, :]
            first = whole.astype(jnp.bfloat16)
            high[s, spot, :] = first
            low[s, spot, :] = (whole - first.astype(jnp.float32)).astype(jnp.bfloat16)
            return carry

        lax.fori_loop(0, tile // PART, split, 0)

    def step(k, carry):
        v = [vecs[k, h] for h in range(blocks)]

        @pl.when(k > 0)
        def _():
            sent(k - 1)

        image = [zero] * blocks
        spill = zero
        for b in range(COMP):
            passed = zero
            for h in range(blocks):
                term = zero
                for a in range(COMP):
                    term = term + band[a, b, h] * v[h][a : a + 1, :]
                turned = pltpu.roll(term, 1, 1, stride=1, stride_axis=0)
                moved = jnp.sum(jnp.where(lane_iota > row_iota, turned, passed), axis=0, keepdims=True)
                image[h] = jnp.where(row_iota == b, moved, image[h])
                passed = turned
            moved = jnp.sum(jnp.where(lane_iota > row_iota, 0.0, passed), axis=0, keepdims=True)
            spill = jnp.where(row_iota == b, moved, spill)
        spill_out[k] = spill
        spill_copy(k).start()

        for copy in row_gathers(k):
            copy.wait_recv()
        col_acc[...] = products(select(pick_row, row_in[k].reshape(nc * slab, lanes)), 0)
        col_out[k] = select(put_col, col_acc[...])
        sums = jnp.zeros((2, lanes), jnp.float32)
        for d in range(nc):
            sums = sums + row_in[k, d, COMP:SUB, :]
        for d in range(nf):
            col_out[k, d * slab + COMP : d * slab + SUB, :] = sums
        for copy in col_returns(k):
            copy.start()
        col_back[k, f] = col_out[k, pl.ds(pl.multiple_of(f * slab, SUB), slab), :]

        halo_copy(k).wait_recv()
        ext = v + [halo_in[k]]
        forward = [[zero] * COMP for _ in range(blocks)]
        for b in range(COMP):
            turned = [
                pltpu.roll(jnp.broadcast_to(part[b : b + 1, :], (SUB, lanes)), lanes - SUB, 1, stride=1, stride_axis=0)
                for part in ext
            ]
            for h in range(blocks):
                moved = jnp.where(lane_iota - row_iota < lanes - SUB, turned[h], turned[h + 1])
                for a in range(COMP):
                    forward[h][a] = forward[h][a] + flipped[a, b, h] * moved
        quad = jnp.zeros((1, lanes), jnp.float32)
        for h in range(blocks):
            ahead = zero
            for a in range(COMP):
                ahead = jnp.where(row_iota == a, jnp.sum(forward[h][a], axis=0, keepdims=True), ahead)
            quad = quad + jnp.sum(ahead * v[h], axis=0, keepdims=True)
            image[h] = image[h] + ahead

        for copy in col_gathers(k):
            copy.wait_recv()
        c_rows = select(pick_col, col_in[k].reshape(nf * slab, lanes))

        @pl.when(k == last)
        def _():
            part = 2.0 * (quad + jnp.sum(col_acc[...] * c_rows, axis=0, keepdims=True))
            quad_out[...] = jnp.broadcast_to(part, (SUB, lanes))
            for copy in quad_copies():
                copy.start()
            quad_in[c] = quad_out[...]

        gains = products(c_rows, 1)

        @pl.when(k == last)
        def _():
            for copy in quad_copies():
                copy.wait_recv()
            last_out[...] = jnp.sum(quad_in[...], axis=0)
            for copy in last_copies():
                copy.start()
            last_in[f] = last_out[...]

        row_out[k] = select(put_row, gains)
        for copy in row_returns(k):
            copy.start()
        row_back[k, c] = row_out[k, pl.ds(pl.multiple_of(c * slab, SUB), slab), :]
        spill_copy(k).wait_recv()
        image[0] = image[0] + spill_in[k]
        for copy in col_returns(k) + row_returns(k):
            copy.wait_recv()
        total = jnp.sum(row_back[k], axis=0) + jnp.sum(col_back[k], axis=0)
        nus[k] = total[0:SUB, :]
        for h in range(blocks):
            part = jnp.where(row_iota < COMP, total[h * SUB : (h + 1) * SUB, :], 0.0)
            image[h] = image[h] + swap_pairs(part, side)
            ys[k + 1, h] = image[h]

        @pl.when(k < last)
        def _():
            for h in range(blocks):
                vecs[k + 1, h] = precondition(h, image[h])
            publish(k + 1)

        return carry

    last = ITERS - 1
    lax.fori_loop(0, ITERS, step, 0)

    moments = []
    for k in range(ITERS):
        if k:
            moments.append(jnp.sum(nus[k, COMP + 1 : COMP + 2, :], axis=1, keepdims=True))
        moments.append(jnp.sum(nus[k, COMP : COMP + 1, :], axis=1, keepdims=True))

    def quadratic(coefs, values):
        sums = {}
        for i, left in enumerate(coefs):
            for j, right in enumerate(coefs):
                sums.setdefault(i + j, []).append(left * right)
        total = None
        for at, terms in sums.items():
            term = sum(terms[1:], terms[0]) * values(at)
            total = term if total is None else total + term
        return total

    one = jnp.ones((1, 1), jnp.float32)
    none = jnp.zeros((1, 1), jnp.float32)
    rho = [one]
    pi = [one]
    xi = []
    gamma = quadratic(rho, lambda at: moments[at])
    for iteration in range(ITERS):
        if iteration == last:
            for copy in last_copies():
                copy.wait_recv()
            ending = jnp.sum(last_in[...], axis=0)[0:1, :]
            moments.append(jnp.sum(ending, axis=1, keepdims=True))
        alpha = gamma / quadratic(pi, lambda at: moments[at] + moments[at + 1])
        xi = [x + alpha * p for x, p in zip(xi + [none] * (len(pi) - len(xi)), pi)]
        image = [(pi[i] if i < len(pi) else none) + (pi[i - 1] if i else none) for i in range(len(pi) + 1)]
        rho = [r - alpha * s for r, s in zip(rho + [none], image)]
        if iteration < last:
            fresh = quadratic(rho, lambda at: moments[at])
            beta = fresh / gamma
            pi = [r + beta * p for r, p in zip(rho, pi + [none])]
            gamma = fresh

    for h in range(blocks):
        cut = slice(h * lanes, (h + 1) * lanes)
        sol = zero
        res = zero
        for k in range(ITERS):
            sol = sol + xi[k] * vecs[k, h]
        for k in range(ITERS + 1):
            res = res + rho[k] * ys[k, h]
        out_ref[0, :, cut] = sol[0:COMP, :]
        out_ref[1, :, cut] = res[0:COMP, :]
    sent(last)
    for copy in quad_copies() + last_copies():
        copy.wait_send()


def per_device(nf, nc, right_side, diag_blocks, band_blocks, reach, tiles, tile_rows, tile_cols, tile_count):
    slots, tile = tiles.shape[2], tiles.shape[3]
    lanes = 2 * (tile // COMP)
    chunks = tile // lanes
    frames = right_side.shape[1]
    blocks = frames // lanes
    slab = blocks * SUB
    reach_len = band_blocks.shape[0]
    padded = -(-slots * chunks // (2 * SUB)) * 2 * SUB
    f32 = jnp.float32
    vmem = pl.BlockSpec(memory_space=pltpu.VMEM)
    dma = pltpu.SemaphoreType.DMA
    bf16 = jnp.bfloat16
    scratch = [
        pltpu.VMEM(right_side.shape, f32),
        pltpu.VMEM(diag_blocks.shape, f32),
        pltpu.VMEM((COMP, COMP, reach_len, frames), f32),
        pltpu.VMEM((1, frames), jnp.int32),
        pltpu.SMEM(tile_rows.shape, jnp.int32),
        pltpu.SMEM(tile_cols.shape, jnp.int32),
        pltpu.SMEM(tile_count.shape, jnp.int32),
        pltpu.VMEM((slots, tile, tile), f32),
        pltpu.VMEM((slots, tile, tile), bf16),
        pltpu.VMEM((slots, tile, tile), bf16),
        pltpu.VMEM((COMP, COMP, blocks, SUB, lanes), f32),
        pltpu.VMEM((COMP, COMP, blocks, SUB, lanes), f32),
        pltpu.VMEM((COMP, blocks, SUB, lanes), f32),
        pltpu.VMEM((ITERS + 1, blocks, SUB, lanes), f32),
        pltpu.VMEM((ITERS + 1, blocks, SUB, lanes), f32),
        pltpu.VMEM((ITERS, nc, slab, lanes), f32),
        pltpu.VMEM((ITERS, nf, slab, lanes), f32),
        pltpu.VMEM((ITERS, SUB, lanes), f32),
        pltpu.VMEM((ITERS, SUB, lanes), f32),
        pltpu.VMEM((ITERS, SUB, lanes), f32),
        pltpu.VMEM((ITERS, nc * slab, lanes), f32),
        pltpu.VMEM((ITERS, nf * slab, lanes), f32),
        pltpu.VMEM((ITERS, nc, slab, lanes), f32),
        pltpu.VMEM((ITERS, nf, slab, lanes), f32),
        pltpu.VMEM((SUB, lanes), f32),
        pltpu.VMEM((nc, SUB, lanes), f32),
        pltpu.VMEM((SUB, lanes), f32),
        pltpu.VMEM((nf, SUB, lanes), f32),
        pltpu.VMEM((padded, 3 * nc * slab), bf16),
        pltpu.VMEM((padded, 3 * nf * slab), bf16),
        pltpu.VMEM((nc * slab, 3 * padded), bf16),
        pltpu.VMEM((nf * slab, 3 * padded), bf16),
        pltpu.VMEM((padded, lanes), f32),
        pltpu.VMEM((ITERS, SUB, lanes), f32),
        dma((slots,)),
        dma((7,)),
    ]
    for shape in ((ITERS, nc), (ITERS, nf), (ITERS,), (ITERS,), (ITERS, nc), (ITERS, nf), (nc,), (nf,)):
        scratch += [dma(shape), dma(shape)]
    out = pl.pallas_call(
        functools.partial(kernel, nf, nc),
        out_shape=jax.ShapeDtypeStruct((2,) + right_side.shape, f32),
        in_specs=[pl.BlockSpec(memory_space=pltpu.HBM)] * 8,
        out_specs=vmem,
        scratch_shapes=scratch,
        compiler_params=pltpu.CompilerParams(
            collective_id=0, has_side_effects=True, vmem_limit_bytes=60 * 1024 * 1024
        ),
        cost_estimate=pl.CostEstimate(
            flops=4 * ITERS * tiles.size, bytes_accessed=4 * (tiles.size + band_blocks.size), transcendentals=0
        ),
    )(right_side, diag_blocks, band_blocks.transpose(1, 2, 0, 3), reach.reshape(1, -1), tiles, tile_rows, tile_cols, tile_count)
    return out[0], out[1]


def solution(mesh):
    return jax.shard_map(
        functools.partial(per_device, mesh.shape["frames"], mesh.shape["cols"]),
        mesh=mesh,
        in_specs=(
            P(None, ("frames", "cols")),
            P(None, None, ("frames", "cols")),
            P(None, None, None, ("frames", "cols")),
            P(("frames", "cols")),
            P("frames", "cols", None, None, None),
            P("frames", "cols", None),
            P("frames", "cols", None),
            P("frames", "cols"),
        ),
        out_specs=(P(None, ("frames", "cols")), P(None, ("frames", "cols"))),
        check_vma=False,
    )
```

```python
import functools

import jax
import jax.numpy as jnp
from jax import lax
from jax.experimental import pallas as pl
from jax.experimental.pallas import tpu as pltpu
from jax.sharding import PartitionSpec as P

ITERS = 4
COMP = 6
SUB = 8
UNROLL = 4
MESH = pl.DeviceIdType.MESH


def swap_pairs(block, side):
    row = lax.broadcasted_iota(jnp.int32, block.shape, 0)
    lane = lax.broadcasted_iota(jnp.int32, block.shape, 1)
    odd = row % 2
    turned = pltpu.roll(block, side, 1)
    above = pltpu.roll(turned, SUB - 1, 0)
    below = pltpu.roll(turned, 1, 0)
    return jnp.where(odd == lane // side, block, jnp.where(odd == 0, above, below))


def flip_rows(block):
    row = lax.broadcasted_iota(jnp.int32, block.shape, 0)
    block = pltpu.roll(block, SUB // 2, 0)
    for step in (2, 1):
        up, down = pltpu.roll(block, SUB - step, 0), pltpu.roll(block, step, 0)
        block = jnp.where((row // step) % 2 == 0, up, down)
    return block


def kernel(
    nf,
    nc,
    rhs_hbm,
    diag_hbm,
    band_hbm,
    reach_hbm,
    tiles_hbm,
    rows_hbm,
    cols_hbm,
    count_hbm,
    out_ref,
    rhs_ref,
    diag_ref,
    band_ref,
    reach_ref,
    rows_ref,
    cols_ref,
    count_ref,
    tiles,
    band,
    flipped,
    inv,
    vecs,
    ys,
    row_in,
    col_in,
    halo_in,
    spill_out,
    spill_in,
    row_out,
    col_out,
    row_back,
    col_back,
    quad_out,
    quad_in,
    last_out,
    last_in,
    pick_row,
    pick_col,
    put_row,
    put_col,
    r_cols,
    c_rows,
    g_cols,
    col_acc,
    nus,
    tile_sem,
    load_sem,
    s_row,
    r_row,
    s_col,
    r_col,
    s_halo,
    r_halo,
    s_spill,
    r_spill,
    s_rowb,
    r_rowb,
    s_colb,
    r_colb,
    s_quad,
    r_quad,
    s_last,
    r_last,
):
    f = lax.axis_index("frames")
    c = lax.axis_index("cols")
    slots, tile, _ = tiles.shape
    side = tile // COMP
    lanes = 2 * side
    chunks = tile // lanes
    blocks = vecs.shape[1]
    frames = blocks * lanes
    slab = blocks * SUB
    reach_len = band_ref.shape[2]

    small = [
        pltpu.make_async_copy(src, dst, load_sem.at[at])
        for at, (src, dst) in enumerate(
            (
                (diag_hbm, diag_ref),
                (rhs_hbm, rhs_ref),
                (rows_hbm, rows_ref),
                (cols_hbm, cols_ref),
                (count_hbm, count_ref),
                (reach_hbm, reach_ref),
                (band_hbm, band_ref),
            )
        )
    ]
    for copy in small:
        copy.start()
    loads = [pltpu.make_async_copy(tiles_hbm.at[0, 0, t], tiles.at[t], tile_sem.at[t]) for t in range(slots)]
    for copy in loads:
        copy.start()

    row_peers = [(f, lax.rem(c + d, nc)) for d in range(1, nc)]
    col_peers = [(lax.rem(f + d, nf), c) for d in range(1, nf)]
    after = (lax.rem(f + (c + 1) // nc, nf), lax.rem(c + 1, nc))
    before = (lax.rem(f + nf - 1 + (c + nc - 1) // nc, nf), lax.rem(c + nc - 1, nc))
    is_first = (f == 0) & (c == 0)
    is_last = (f == nf - 1) & (c == nc - 1)
    barrier = pltpu.get_barrier_semaphore()

    def greet(peer):
        pl.semaphore_signal(barrier, inc=1, device_id=peer, device_id_type=MESH)

    for peer in col_peers + row_peers:
        greet(peer)

    @pl.when(jnp.logical_not(is_first))
    def _():
        greet(before)

    @pl.when(jnp.logical_not(is_last))
    def _():
        greet(after)

    @pl.when(is_first)
    def _():
        spill_in[...] = jnp.zeros_like(spill_in)

    @pl.when(is_last)
    def _():
        halo_in[...] = jnp.zeros_like(halo_in)

    row_iota = lax.broadcasted_iota(jnp.int32, (SUB, lanes), 0)
    lane_iota = lax.broadcasted_iota(jnp.int32, (SUB, lanes), 1)
    zero = jnp.zeros((SUB, lanes), jnp.float32)

    ys[0] = jnp.zeros((blocks, SUB, lanes), jnp.float32)
    inv[...] = jnp.zeros_like(inv)
    for copy in small[:2]:
        copy.wait()
    for h in range(blocks):
        cut = slice(h * lanes, (h + 1) * lanes)
        ys[0, h, 0:COMP, :] = rhs_ref[:, cut]
        for a in range(COMP):
            inv[a, h, 0:COMP, :] = diag_ref[a, :, cut]
    for h in range(blocks):
        mat = [inv[a, h] for a in range(COMP)]
        out = [jnp.where(row_iota == a, 1.0, 0.0) for a in range(COMP)]
        for p in range(COMP):
            pivot = mat[p][p : p + 1, :]
            mat[p] = mat[p] / pivot
            out[p] = out[p] / pivot
            for a in range(COMP):
                if a != p:
                    factor = mat[a][p : p + 1, :]
                    mat[a] = mat[a] - factor * mat[p]
                    out[a] = out[a] - factor * out[p]
        for a in range(COMP):
            inv[a, h] = out[a]

    def precondition(h, value):
        total = zero
        for a in range(COMP):
            total = total + inv[a, h] * value[a : a + 1, :]
        return total

    for h in range(blocks):
        vecs[0, h] = precondition(h, ys[0, h])

    ends = jnp.where(is_first, 1, 0) + jnp.where(is_last, 1, 0)
    pl.semaphore_wait(barrier, len(col_peers) + len(row_peers) + 2 - ends)

    def unless(edge, act):
        @pl.when(jnp.logical_not(edge))
        def _():
            act()

    def remote(src, dst, send, recv, peer):
        return pltpu.make_async_remote_copy(
            src_ref=src, dst_ref=dst, send_sem=send, recv_sem=recv, device_id=peer, device_id_type=MESH
        )

    def row_gathers(k):
        return [
            remote(row_in.at[k, c], row_in.at[k, c], s_row.at[k, d], r_row.at[k, d], row_peers[d - 1])
            for d in range(1, nc)
        ]

    def col_gathers(k):
        return [
            remote(col_in.at[k, f], col_in.at[k, f], s_col.at[k, d], r_col.at[k, d], col_peers[d - 1])
            for d in range(1, nf)
        ]

    def halo_copy(k):
        return remote(vecs.at[k, 0], halo_in.at[k], s_halo.at[k], r_halo.at[k], before)

    def spill_copy(k):
        return remote(spill_out.at[k], spill_in.at[k], s_spill.at[k], r_spill.at[k], after)

    def col_returns(k):
        copies = []
        for d in range(1, nf):
            peer = col_peers[d - 1]
            part = col_out.at[k, pl.ds(pl.multiple_of(peer[0] * slab, SUB), slab), :]
            copies.append(remote(part, col_back.at[k, f], s_colb.at[k, d], r_colb.at[k, d], peer))
        return copies

    def row_returns(k):
        copies = []
        for d in range(1, nc):
            peer = row_peers[d - 1]
            part = row_out.at[k, pl.ds(pl.multiple_of(peer[1] * slab, SUB), slab), :]
            copies.append(remote(part, row_back.at[k, c], s_rowb.at[k, d], r_rowb.at[k, d], peer))
        return copies

    def quad_copies():
        return [remote(quad_out, quad_in.at[c], s_quad.at[d], r_quad.at[d], row_peers[d - 1]) for d in range(1, nc)]

    def last_copies():
        return [remote(last_out, last_in.at[f], s_last.at[d], r_last.at[d], col_peers[d - 1]) for d in range(1, nf)]

    def sent(k):
        for copy in row_gathers(k) + col_gathers(k) + col_returns(k) + row_returns(k):
            copy.wait_send()
        unless(is_first, lambda: halo_copy(k).wait_send())
        unless(is_last, lambda: spill_copy(k).wait_send())

    def publish(k):
        prev = jnp.maximum(k - 1, 0)
        even = jnp.zeros((1, lanes), jnp.float32)
        odd = jnp.zeros((1, lanes), jnp.float32)
        for h in range(blocks):
            y = ys[k, h]
            even = even + jnp.sum(vecs[k, h] * y, axis=0, keepdims=True)
            odd = odd + jnp.sum(vecs[prev, h] * y, axis=0, keepdims=True)
        paired = [swap_pairs(vecs[k, h], side) for h in range(blocks)]
        paired[0] = jnp.where(row_iota == COMP, even, jnp.where(row_iota == COMP + 1, odd, paired[0]))
        for h in range(blocks):
            row_in[k, c, h * SUB : (h + 1) * SUB, :] = paired[h]
            col_in[k, f, h * SUB : (h + 1) * SUB, :] = paired[h]
        for copy in row_gathers(k) + col_gathers(k):
            copy.start()
        unless(is_first, lambda: halo_copy(k).start())

    publish(0)

    for copy in small[2:]:
        copy.wait()

    limit = jnp.where(is_last, frames, frames + reach_len)
    for h in range(blocks):
        cut = slice(h * lanes, (h + 1) * lanes)
        offset = row_iota + 1
        keep = (offset <= reach_ref[:, cut]) & (lane_iota + h * lanes + offset < limit)
        keep = jnp.where(keep, 1.0, 0.0)
        for a in range(COMP):
            for b in range(COMP):
                block = band_ref[a, b, :, cut] * keep
                band[a, b, h] = block
                flipped[a, b, h] = flip_rows(block)

    count = count_ref[0, 0]

    def targets(ids_ref, iota, width):
        out = jnp.full(iota.shape, -1, jnp.int32)
        slot_at = iota // width
        for s in range(slots):
            at = ids_ref[0, 0, s]
            base = jnp.where(s < count, (at // 2) * SUB + lax.rem(at, 2), -slab * nf * nc)
            for j in range(chunks):
                out = jnp.where(slot_at == j * slots + s, base + 2 * j, out)
        return out

    for ids, pick, put, width in ((rows_ref, pick_row, put_row, 1), (cols_ref, pick_col, put_col, SUB)):
        rows, wide = pick.shape[0], pick.shape[1] // 3
        down = targets(ids, lax.broadcasted_iota(jnp.int32, (rows, 1), 0), 1)
        once = jnp.where(lax.broadcasted_iota(jnp.int32, (rows, wide), 1) == down, 1.0, 0.0)
        pick[...] = jnp.concatenate([once] * 3, axis=1).astype(jnp.bfloat16)
        rows, wide = put.shape[0], put.shape[1] // 3
        along = targets(ids, lax.broadcasted_iota(jnp.int32, (1, wide), 1), width)
        once = jnp.where(lax.broadcasted_iota(jnp.int32, (rows, wide), 0) == along, 1.0, 0.0)
        put[...] = jnp.concatenate([once] * 3, axis=1).astype(jnp.bfloat16)

    def select(pick, value):
        first = value.astype(jnp.bfloat16)
        left = value - first.astype(jnp.float32)
        second = left.astype(jnp.bfloat16)
        third = (left - second.astype(jnp.float32)).astype(jnp.bfloat16)
        parts = jnp.concatenate([first, second, third], axis=0)
        return jnp.dot(pick[...], parts, preferred_element_type=jnp.float32)

    def step(k, carry):
        v = [vecs[k, h] for h in range(blocks)]

        @pl.when(k > 0)
        def _():
            sent(k - 1)

        image = [zero] * blocks
        spill = zero
        for b in range(COMP):
            passed = zero
            for h in range(blocks):
                term = zero
                for a in range(COMP):
                    term = term + band[a, b, h] * v[h][a : a + 1, :]
                turned = pltpu.roll(term, 1, 1, stride=1, stride_axis=0)
                moved = jnp.sum(jnp.where(lane_iota > row_iota, turned, passed), axis=0, keepdims=True)
                image[h] = jnp.where(row_iota == b, moved, image[h])
                passed = turned
            moved = jnp.sum(jnp.where(lane_iota > row_iota, 0.0, passed), axis=0, keepdims=True)
            spill = jnp.where(row_iota == b, moved, spill)
        spill_out[k] = spill
        unless(is_last, lambda: spill_copy(k).start())

        for copy in row_gathers(k):
            copy.wait_recv()
        rows_all = row_in[k].reshape(nc * slab, lanes)
        r_cols[...] = select(pick_row, rows_all).T

        @pl.when(k == 0)
        def _():
            for copy in loads:
                copy.wait()

        def transposed(i, accs):
            accs = list(accs)
            for u in range(UNROLL):
                at = pl.multiple_of(i * (SUB * UNROLL) + u * SUB, SUB)
                r_now = r_cols[pl.ds(at, SUB), :]
                for s in range(slots):
                    for j in range(chunks):
                        col = j * slots + s
                        spot = pl.multiple_of(j * lanes + at, SUB)
                        x = jnp.broadcast_to(r_now[:, col : col + 1], (SUB, lanes))
                        for n in range(chunks):
                            part = tiles[s, pl.ds(spot, SUB), n * lanes : (n + 1) * lanes]
                            accs[n * slots + s] = accs[n * slots + s] + part * x
            return tuple(accs)

        accs = lax.fori_loop(0, lanes // (SUB * UNROLL), transposed, (zero,) * (slots * chunks))
        for q, acc in enumerate(accs):
            col_acc[q * SUB : (q + 1) * SUB, :] = acc
        col_out[k] = select(put_col, col_acc[...])
        sums = jnp.zeros((2, lanes), jnp.float32)
        for d in range(nc):
            sums = sums + row_in[k, d, COMP:SUB, :]
        for d in range(nf):
            col_out[k, d * slab + COMP : d * slab + SUB, :] = sums
        for copy in col_returns(k):
            copy.start()
        col_back[k, f] = col_out[k, pl.ds(pl.multiple_of(f * slab, SUB), slab), :]

        unless(is_last, lambda: halo_copy(k).wait_recv())
        ext = v + [halo_in[k]]
        forward = [[zero] * COMP for _ in range(blocks)]
        for b in range(COMP):
            turned = [
                pltpu.roll(jnp.broadcast_to(part[b : b + 1, :], (SUB, lanes)), lanes - SUB, 1, stride=1, stride_axis=0)
                for part in ext
            ]
            for h in range(blocks):
                moved = jnp.where(lane_iota - row_iota < lanes - SUB, turned[h], turned[h + 1])
                for a in range(COMP):
                    forward[h][a] = forward[h][a] + flipped[a, b, h] * moved
        quad = jnp.zeros((1, lanes), jnp.float32)
        for h in range(blocks):
            ahead = zero
            for a in range(COMP):
                ahead = jnp.where(row_iota == a, jnp.sum(forward[h][a], axis=0, keepdims=True), ahead)
            quad = quad + jnp.sum(ahead * v[h], axis=0, keepdims=True)
            image[h] = image[h] + ahead

        for copy in col_gathers(k):
            copy.wait_recv()
        cols_all = col_in[k].reshape(nf * slab, lanes)
        c_rows[...] = select(pick_col, cols_all)

        @pl.when(k == last)
        def _():
            both = zero
            for q in range(slots * chunks):
                both = both + col_acc[q * SUB : (q + 1) * SUB, :] * c_rows[q : q + 1, :]
            part = 2.0 * (quad + jnp.sum(both, axis=0, keepdims=True))
            quad_out[...] = jnp.broadcast_to(part, (SUB, lanes))
            for copy in quad_copies():
                copy.start()
            quad_in[c] = quad_out[...]

        def direct(i, carry):
            for u in range(UNROLL):
                at = pl.multiple_of(i * (SUB * UNROLL) + u * SUB, SUB)
                g_now = zero
                for s in range(slots):
                    for j in range(chunks):
                        spot = pl.multiple_of(j * lanes + at, SUB)
                        dots = None
                        for n in range(chunks):
                            part = tiles[s, pl.ds(spot, SUB), n * lanes : (n + 1) * lanes]
                            here = n * slots + s
                            term = part * c_rows[here : here + 1, :]
                            dots = term if dots is None else dots + term
                        g_now = jnp.where(
                            lane_iota == j * slots + s, jnp.sum(dots, axis=1, keepdims=True), g_now
                        )
                g_cols[pl.ds(at, SUB), :] = g_now
            return carry

        lax.fori_loop(0, lanes // (SUB * UNROLL), direct, 0)

        @pl.when(k == last)
        def _():
            for copy in quad_copies():
                copy.wait_recv()
            last_out[...] = jnp.sum(quad_in[...], axis=0)
            for copy in last_copies():
                copy.start()
            last_in[f] = last_out[...]

        row_out[k] = select(put_row, g_cols[...].T)
        for copy in row_returns(k):
            copy.start()
        row_back[k, c] = row_out[k, pl.ds(pl.multiple_of(c * slab, SUB), slab), :]
        unless(is_first, lambda: spill_copy(k).wait_recv())
        image[0] = image[0] + spill_in[k]
        for copy in col_returns(k) + row_returns(k):
            copy.wait_recv()
        total = jnp.sum(row_back[k], axis=0) + jnp.sum(col_back[k], axis=0)
        nus[k] = total[0:SUB, :]
        for h in range(blocks):
            part = jnp.where(row_iota < COMP, total[h * SUB : (h + 1) * SUB, :], 0.0)
            image[h] = image[h] + swap_pairs(part, side)
            ys[k + 1, h] = image[h]

        @pl.when(k < last)
        def _():
            for h in range(blocks):
                vecs[k + 1, h] = precondition(h, image[h])
            publish(k + 1)

        return carry

    last = ITERS - 1
    lax.fori_loop(0, ITERS, step, 0)

    moments = []
    for k in range(ITERS):
        if k:
            moments.append(jnp.sum(nus[k, COMP + 1 : COMP + 2, :], axis=1, keepdims=True))
        moments.append(jnp.sum(nus[k, COMP : COMP + 1, :], axis=1, keepdims=True))

    def quadratic(coefs, values):
        sums = {}
        for i, left in enumerate(coefs):
            for j, right in enumerate(coefs):
                sums.setdefault(i + j, []).append(left * right)
        total = None
        for at, terms in sums.items():
            term = sum(terms[1:], terms[0]) * values(at)
            total = term if total is None else total + term
        return total

    one = jnp.ones((1, 1), jnp.float32)
    none = jnp.zeros((1, 1), jnp.float32)
    rho = [one]
    pi = [one]
    xi = []
    gamma = quadratic(rho, lambda at: moments[at])
    for iteration in range(ITERS):
        if iteration == last:
            for copy in last_copies():
                copy.wait_recv()
            ending = jnp.sum(last_in[...], axis=0)[0:1, :]
            moments.append(jnp.sum(ending, axis=1, keepdims=True))
        alpha = gamma / quadratic(pi, lambda at: moments[at] + moments[at + 1])
        xi = [x + alpha * p for x, p in zip(xi + [none] * (len(pi) - len(xi)), pi)]
        image = [(pi[i] if i < len(pi) else none) + (pi[i - 1] if i else none) for i in range(len(pi) + 1)]
        rho = [r - alpha * s for r, s in zip(rho + [none], image)]
        if iteration < last:
            fresh = quadratic(rho, lambda at: moments[at])
            beta = fresh / gamma
            pi = [r + beta * p for r, p in zip(rho, pi + [none])]
            gamma = fresh

    for h in range(blocks):
        cut = slice(h * lanes, (h + 1) * lanes)
        sol = zero
        res = zero
        for k in range(ITERS):
            sol = sol + xi[k] * vecs[k, h]
        for k in range(ITERS + 1):
            res = res + rho[k] * ys[k, h]
        out_ref[0, :, cut] = sol[0:COMP, :]
        out_ref[1, :, cut] = res[0:COMP, :]
    sent(last)
    for copy in quad_copies() + last_copies():
        copy.wait_send()


def per_device(nf, nc, right_side, diag_blocks, band_blocks, reach, tiles, tile_rows, tile_cols, tile_count):
    slots, tile = tiles.shape[2], tiles.shape[3]
    lanes = 2 * (tile // COMP)
    chunks = tile // lanes
    frames = right_side.shape[1]
    blocks = frames // lanes
    slab = blocks * SUB
    reach_len = band_blocks.shape[0]
    padded = -(-slots * chunks // lanes) * lanes
    f32 = jnp.float32
    vmem = pl.BlockSpec(memory_space=pltpu.VMEM)
    dma = pltpu.SemaphoreType.DMA
    bf16 = jnp.bfloat16
    scratch = [
        pltpu.VMEM(right_side.shape, f32),
        pltpu.VMEM(diag_blocks.shape, f32),
        pltpu.VMEM((COMP, COMP, reach_len, frames), f32),
        pltpu.VMEM((1, frames), jnp.int32),
        pltpu.SMEM(tile_rows.shape, jnp.int32),
        pltpu.SMEM(tile_cols.shape, jnp.int32),
        pltpu.SMEM(tile_count.shape, jnp.int32),
        pltpu.VMEM((slots, tile, tile), f32),
        pltpu.VMEM((COMP, COMP, blocks, SUB, lanes), f32),
        pltpu.VMEM((COMP, COMP, blocks, SUB, lanes), f32),
        pltpu.VMEM((COMP, blocks, SUB, lanes), f32),
        pltpu.VMEM((ITERS + 1, blocks, SUB, lanes), f32),
        pltpu.VMEM((ITERS + 1, blocks, SUB, lanes), f32),
        pltpu.VMEM((ITERS, nc, slab, lanes), f32),
        pltpu.VMEM((ITERS, nf, slab, lanes), f32),
        pltpu.VMEM((ITERS, SUB, lanes), f32),
        pltpu.VMEM((ITERS, SUB, lanes), f32),
        pltpu.VMEM((ITERS, SUB, lanes), f32),
        pltpu.VMEM((ITERS, nc * slab, lanes), f32),
        pltpu.VMEM((ITERS, nf * slab, lanes), f32),
        pltpu.VMEM((ITERS, nc, slab, lanes), f32),
        pltpu.VMEM((ITERS, nf, slab, lanes), f32),
        pltpu.VMEM((SUB, lanes), f32),
        pltpu.VMEM((nc, SUB, lanes), f32),
        pltpu.VMEM((SUB, lanes), f32),
        pltpu.VMEM((nf, SUB, lanes), f32),
        pltpu.VMEM((padded, 3 * nc * slab), bf16),
        pltpu.VMEM((padded, 3 * nf * slab), bf16),
        pltpu.VMEM((nc * slab, 3 * padded), bf16),
        pltpu.VMEM((nf * slab, 3 * slots * chunks * SUB), bf16),
        pltpu.VMEM((lanes, padded), f32),
        pltpu.VMEM((padded, lanes), f32),
        pltpu.VMEM((lanes, padded), f32),
        pltpu.VMEM((slots * chunks * SUB, lanes), f32),
        pltpu.VMEM((ITERS, SUB, lanes), f32),
        dma((slots,)),
        dma((7,)),
    ]
    for shape in ((ITERS, nc), (ITERS, nf), (ITERS,), (ITERS,), (ITERS, nc), (ITERS, nf), (nc,), (nf,)):
        scratch += [dma(shape), dma(shape)]
    out = pl.pallas_call(
        functools.partial(kernel, nf, nc),
        out_shape=jax.ShapeDtypeStruct((2,) + right_side.shape, f32),
        in_specs=[pl.BlockSpec(memory_space=pltpu.HBM)] * 8,
        out_specs=vmem,
        scratch_shapes=scratch,
        compiler_params=pltpu.CompilerParams(
            collective_id=0, has_side_effects=True, vmem_limit_bytes=60 * 1024 * 1024
        ),
        cost_estimate=pl.CostEstimate(
            flops=4 * ITERS * tiles.size, bytes_accessed=4 * (tiles.size + band_blocks.size), transcendentals=0
        ),
    )(right_side, diag_blocks, band_blocks.transpose(1, 2, 0, 3), reach.reshape(1, -1), tiles, tile_rows, tile_cols, tile_count)
    return out[0], out[1]


def solution(mesh):
    return jax.shard_map(
        functools.partial(per_device, mesh.shape["frames"], mesh.shape["cols"]),
        mesh=mesh,
        in_specs=(
            P(None, ("frames", "cols")),
            P(None, None, ("frames", "cols")),
            P(None, None, None, ("frames", "cols")),
            P(("frames", "cols")),
            P("frames", "cols", None, None, None),
            P("frames", "cols", None),
            P("frames", "cols", None),
            P("frames", "cols"),
        ),
        out_specs=(P(None, ("frames", "cols")), P(None, ("frames", "cols"))),
        check_vma=False,
    )
```

```python
import functools

import jax
import jax.numpy as jnp
from jax import lax
from jax.experimental import pallas as pl
from jax.experimental.pallas import tpu as pltpu
from jax.sharding import PartitionSpec as P

ITERS = 4
COMP = 6
SUB = 8
UNROLL = 4
MESH = pl.DeviceIdType.MESH


def swap_pairs(block, side):
    row = lax.broadcasted_iota(jnp.int32, block.shape, 0)
    lane = lax.broadcasted_iota(jnp.int32, block.shape, 1)
    odd = row % 2
    turned = pltpu.roll(block, side, 1)
    above = pltpu.roll(turned, SUB - 1, 0)
    below = pltpu.roll(turned, 1, 0)
    return jnp.where(odd == lane // side, block, jnp.where(odd == 0, above, below))


def flip_rows(block):
    row = lax.broadcasted_iota(jnp.int32, block.shape, 0)
    block = pltpu.roll(block, SUB // 2, 0)
    for step in (2, 1):
        up, down = pltpu.roll(block, SUB - step, 0), pltpu.roll(block, step, 0)
        block = jnp.where((row // step) % 2 == 0, up, down)
    return block


def kernel(
    nf,
    nc,
    rhs_hbm,
    diag_hbm,
    band_hbm,
    reach_hbm,
    tiles_hbm,
    rows_hbm,
    cols_hbm,
    count_hbm,
    out_ref,
    rhs_ref,
    diag_ref,
    band_ref,
    reach_ref,
    rows_ref,
    cols_ref,
    count_ref,
    tiles,
    band,
    flipped,
    inv,
    vecs,
    ys,
    row_in,
    col_in,
    halo_in,
    spill_out,
    spill_in,
    row_out,
    col_out,
    row_back,
    col_back,
    quad_out,
    quad_in,
    last_out,
    last_in,
    pick_row,
    pick_col,
    put_row,
    put_col,
    r_cols,
    c_rows,
    g_cols,
    col_acc,
    nus,
    tile_sem,
    load_sem,
    s_row,
    r_row,
    s_col,
    r_col,
    s_halo,
    r_halo,
    s_spill,
    r_spill,
    s_rowb,
    r_rowb,
    s_colb,
    r_colb,
    s_quad,
    r_quad,
    s_last,
    r_last,
):
    f = lax.axis_index("frames")
    c = lax.axis_index("cols")
    slots, tile, _ = tiles.shape
    side = tile // COMP
    lanes = 2 * side
    chunks = tile // lanes
    blocks = vecs.shape[1]
    frames = blocks * lanes
    slab = blocks * SUB
    reach_len = band_ref.shape[2]

    small = [
        pltpu.make_async_copy(src, dst, load_sem.at[at])
        for at, (src, dst) in enumerate(
            (
                (diag_hbm, diag_ref),
                (rhs_hbm, rhs_ref),
                (rows_hbm, rows_ref),
                (cols_hbm, cols_ref),
                (count_hbm, count_ref),
                (reach_hbm, reach_ref),
                (band_hbm, band_ref),
            )
        )
    ]
    for copy in small:
        copy.start()
    loads = [pltpu.make_async_copy(tiles_hbm.at[0, 0, t], tiles.at[t], tile_sem.at[t]) for t in range(slots)]
    for copy in loads:
        copy.start()

    row_peers = [(f, lax.rem(c + d, nc)) for d in range(1, nc)]
    col_peers = [(lax.rem(f + d, nf), c) for d in range(1, nf)]
    after = (lax.rem(f + (c + 1) // nc, nf), lax.rem(c + 1, nc))
    before = (lax.rem(f + nf - 1 + (c + nc - 1) // nc, nf), lax.rem(c + nc - 1, nc))
    is_first = (f == 0) & (c == 0)
    is_last = (f == nf - 1) & (c == nc - 1)
    barrier = pltpu.get_barrier_semaphore()

    def greet(peer):
        pl.semaphore_signal(barrier, inc=1, device_id=peer, device_id_type=MESH)

    for peer in col_peers + row_peers:
        greet(peer)

    @pl.when(jnp.logical_not(is_first))
    def _():
        greet(before)

    @pl.when(jnp.logical_not(is_last))
    def _():
        greet(after)

    @pl.when(is_first)
    def _():
        spill_in[...] = jnp.zeros_like(spill_in)

    @pl.when(is_last)
    def _():
        halo_in[...] = jnp.zeros_like(halo_in)

    row_iota = lax.broadcasted_iota(jnp.int32, (SUB, lanes), 0)
    lane_iota = lax.broadcasted_iota(jnp.int32, (SUB, lanes), 1)
    zero = jnp.zeros((SUB, lanes), jnp.float32)

    ys[0] = jnp.zeros((blocks, SUB, lanes), jnp.float32)
    inv[...] = jnp.zeros_like(inv)
    for copy in small[:2]:
        copy.wait()
    for h in range(blocks):
        cut = slice(h * lanes, (h + 1) * lanes)
        ys[0, h, 0:COMP, :] = rhs_ref[:, cut]
        for a in range(COMP):
            inv[a, h, 0:COMP, :] = diag_ref[a, :, cut]
    for h in range(blocks):
        mat = [inv[a, h] for a in range(COMP)]
        out = [jnp.where(row_iota == a, 1.0, 0.0) for a in range(COMP)]
        for p in range(COMP):
            pivot = mat[p][p : p + 1, :]
            mat[p] = mat[p] / pivot
            out[p] = out[p] / pivot
            for a in range(COMP):
                if a != p:
                    factor = mat[a][p : p + 1, :]
                    mat[a] = mat[a] - factor * mat[p]
                    out[a] = out[a] - factor * out[p]
        for a in range(COMP):
            inv[a, h] = out[a]

    def precondition(h, value):
        total = zero
        for a in range(COMP):
            total = total + inv[a, h] * value[a : a + 1, :]
        return total

    for h in range(blocks):
        vecs[0, h] = precondition(h, ys[0, h])

    ends = jnp.where(is_first, 1, 0) + jnp.where(is_last, 1, 0)
    pl.semaphore_wait(barrier, len(col_peers) + len(row_peers) + 2 - ends)

    def unless(edge, act):
        @pl.when(jnp.logical_not(edge))
        def _():
            act()

    def remote(src, dst, send, recv, peer):
        return pltpu.make_async_remote_copy(
            src_ref=src, dst_ref=dst, send_sem=send, recv_sem=recv, device_id=peer, device_id_type=MESH
        )

    def row_gathers(k):
        return [
            remote(row_in.at[k, c], row_in.at[k, c], s_row.at[k, d], r_row.at[k, d], row_peers[d - 1])
            for d in range(1, nc)
        ]

    def col_gathers(k):
        return [
            remote(col_in.at[k, f], col_in.at[k, f], s_col.at[k, d], r_col.at[k, d], col_peers[d - 1])
            for d in range(1, nf)
        ]

    def halo_copy(k):
        return remote(vecs.at[k, 0], halo_in.at[k], s_halo.at[k], r_halo.at[k], before)

    def spill_copy(k):
        return remote(spill_out.at[k], spill_in.at[k], s_spill.at[k], r_spill.at[k], after)

    def col_returns(k):
        copies = []
        for d in range(1, nf):
            peer = col_peers[d - 1]
            part = col_out.at[k, pl.ds(pl.multiple_of(peer[0] * slab, SUB), slab), :]
            copies.append(remote(part, col_back.at[k, f], s_colb.at[k, d], r_colb.at[k, d], peer))
        return copies

    def row_returns(k):
        copies = []
        for d in range(1, nc):
            peer = row_peers[d - 1]
            part = row_out.at[k, pl.ds(pl.multiple_of(peer[1] * slab, SUB), slab), :]
            copies.append(remote(part, row_back.at[k, c], s_rowb.at[k, d], r_rowb.at[k, d], peer))
        return copies

    def quad_copies():
        return [remote(quad_out, quad_in.at[c], s_quad.at[d], r_quad.at[d], row_peers[d - 1]) for d in range(1, nc)]

    def last_copies():
        return [remote(last_out, last_in.at[f], s_last.at[d], r_last.at[d], col_peers[d - 1]) for d in range(1, nf)]

    def sent(k):
        for copy in row_gathers(k) + col_gathers(k) + col_returns(k) + row_returns(k):
            copy.wait_send()
        unless(is_first, lambda: halo_copy(k).wait_send())
        unless(is_last, lambda: spill_copy(k).wait_send())

    def publish(k):
        prev = jnp.maximum(k - 1, 0)
        even = jnp.zeros((1, lanes), jnp.float32)
        odd = jnp.zeros((1, lanes), jnp.float32)
        for h in range(blocks):
            y = ys[k, h]
            even = even + jnp.sum(vecs[k, h] * y, axis=0, keepdims=True)
            odd = odd + jnp.sum(vecs[prev, h] * y, axis=0, keepdims=True)
        paired = [swap_pairs(vecs[k, h], side) for h in range(blocks)]
        paired[0] = jnp.where(row_iota == COMP, even, jnp.where(row_iota == COMP + 1, odd, paired[0]))
        for h in range(blocks):
            row_in[k, c, h * SUB : (h + 1) * SUB, :] = paired[h]
            col_in[k, f, h * SUB : (h + 1) * SUB, :] = paired[h]
        for copy in row_gathers(k) + col_gathers(k):
            copy.start()
        unless(is_first, lambda: halo_copy(k).start())

    publish(0)

    for copy in small[2:]:
        copy.wait()

    limit = jnp.where(is_last, frames, frames + reach_len)
    for h in range(blocks):
        cut = slice(h * lanes, (h + 1) * lanes)
        offset = row_iota + 1
        keep = (offset <= reach_ref[:, cut]) & (lane_iota + h * lanes + offset < limit)
        keep = jnp.where(keep, 1.0, 0.0)
        for a in range(COMP):
            for b in range(COMP):
                block = band_ref[a, b, :, cut] * keep
                band[a, b, h] = block
                flipped[a, b, h] = flip_rows(block)

    count = count_ref[0, 0]

    def targets(ids_ref, iota):
        out = jnp.full(iota.shape, -1, jnp.int32)
        for s in range(slots):
            at = ids_ref[0, 0, s]
            base = jnp.where(s < count, (at // 2) * SUB + lax.rem(at, 2), -slab * nf * nc)
            for j in range(chunks):
                out = jnp.where(iota == j * slots + s, base + 2 * j, out)
        return out

    for ids, pick, put in ((rows_ref, pick_row, put_row), (cols_ref, pick_col, put_col)):
        rows, wide = pick.shape[0], pick.shape[1] // 2
        down = targets(ids, lax.broadcasted_iota(jnp.int32, (rows, 1), 0))
        once = jnp.where(lax.broadcasted_iota(jnp.int32, (rows, wide), 1) == down, 1.0, 0.0)
        pick[...] = jnp.concatenate([once] * 2, axis=1).astype(jnp.bfloat16)
        rows, wide = put.shape[0], put.shape[1] // 2
        along = targets(ids, lax.broadcasted_iota(jnp.int32, (1, wide), 1))
        once = jnp.where(lax.broadcasted_iota(jnp.int32, (rows, wide), 0) == along, 1.0, 0.0)
        put[...] = jnp.concatenate([once] * 2, axis=1).astype(jnp.bfloat16)

    def select(pick, value):
        first = value.astype(jnp.bfloat16)
        second = (value - first.astype(jnp.float32)).astype(jnp.bfloat16)
        parts = jnp.concatenate([first, second], axis=0)
        return jnp.dot(pick[...], parts, preferred_element_type=jnp.float32)

    slot_row = lax.broadcasted_iota(jnp.int32, (slots, lanes), 0)

    def step(k, carry):
        v = [vecs[k, h] for h in range(blocks)]

        @pl.when(k > 0)
        def _():
            sent(k - 1)

        image = [zero] * blocks
        spill = zero
        for b in range(COMP):
            passed = zero
            for h in range(blocks):
                term = zero
                for a in range(COMP):
                    term = term + band[a, b, h] * v[h][a : a + 1, :]
                turned = pltpu.roll(term, 1, 1, stride=1, stride_axis=0)
                moved = jnp.sum(jnp.where(lane_iota > row_iota, turned, passed), axis=0, keepdims=True)
                image[h] = jnp.where(row_iota == b, moved, image[h])
                passed = turned
            moved = jnp.sum(jnp.where(lane_iota > row_iota, 0.0, passed), axis=0, keepdims=True)
            spill = jnp.where(row_iota == b, moved, spill)
        spill_out[k] = spill
        unless(is_last, lambda: spill_copy(k).start())

        for copy in row_gathers(k):
            copy.wait_recv()
        rows_all = row_in[k].reshape(nc * slab, lanes)
        r_cols[...] = select(pick_row, rows_all).T

        @pl.when(k == 0)
        def _():
            for copy in loads:
                copy.wait()

        def transposed(i, accs):
            accs = list(accs)
            at = [pl.multiple_of((i * UNROLL + u) * SUB, SUB) for u in range(UNROLL)]
            r_now = [r_cols[pl.ds(at[u], SUB), :] for u in range(UNROLL)]
            for s in range(slots):
                for u in range(UNROLL):
                    for j in range(chunks):
                        col = j * slots + s
                        spot = pl.multiple_of(j * lanes + at[u], SUB)
                        x = jnp.broadcast_to(r_now[u][:, col : col + 1], (SUB, lanes))
                        for n in range(chunks):
                            part = tiles[s, pl.ds(spot, SUB), n * lanes : (n + 1) * lanes]
                            accs[n * slots + s] = accs[n * slots + s] + part * x
            return tuple(accs)

        accs = lax.fori_loop(0, lanes // (SUB * UNROLL), transposed, (zero,) * (slots * chunks))
        col_acc[...] = jnp.zeros_like(col_acc)
        for n in range(chunks):
            folded = jnp.zeros((slots, lanes), jnp.float32)
            for s in range(slots):
                summed = jnp.sum(accs[n * slots + s], axis=0, keepdims=True)
                folded = jnp.where(slot_row == s, summed, folded)
            col_acc[n * slots : (n + 1) * slots, :] = folded
        col_out[k] = select(put_col, col_acc[...])
        sums = jnp.zeros((2, lanes), jnp.float32)
        for d in range(nc):
            sums = sums + row_in[k, d, COMP:SUB, :]
        for d in range(nf):
            col_out[k, d * slab + COMP : d * slab + SUB, :] = sums
        for copy in col_returns(k):
            copy.start()
        col_back[k, f] = col_out[k, pl.ds(pl.multiple_of(f * slab, SUB), slab), :]

        unless(is_last, lambda: halo_copy(k).wait_recv())
        ext = v + [halo_in[k]]
        forward = [[zero] * COMP for _ in range(blocks)]
        for b in range(COMP):
            turned = [
                pltpu.roll(jnp.broadcast_to(part[b : b + 1, :], (SUB, lanes)), lanes - SUB, 1, stride=1, stride_axis=0)
                for part in ext
            ]
            for h in range(blocks):
                moved = jnp.where(lane_iota - row_iota < lanes - SUB, turned[h], turned[h + 1])
                for a in range(COMP):
                    forward[h][a] = forward[h][a] + flipped[a, b, h] * moved
        quad = jnp.zeros((1, lanes), jnp.float32)
        for h in range(blocks):
            ahead = zero
            for a in range(COMP):
                ahead = jnp.where(row_iota == a, jnp.sum(forward[h][a], axis=0, keepdims=True), ahead)
            quad = quad + jnp.sum(ahead * v[h], axis=0, keepdims=True)
            image[h] = image[h] + ahead

        for copy in col_gathers(k):
            copy.wait_recv()
        cols_all = col_in[k].reshape(nf * slab, lanes)
        c_rows[...] = select(pick_col, cols_all)

        @pl.when(k == last)
        def _():
            part = 2.0 * (quad + jnp.sum(col_acc[...] * c_rows[...], axis=0, keepdims=True))
            quad_out[...] = jnp.broadcast_to(part, (SUB, lanes))
            for copy in quad_copies():
                copy.start()
            quad_in[c] = quad_out[...]

        def direct(i, carry):
            at = [pl.multiple_of((i * UNROLL + u) * SUB, SUB) for u in range(UNROLL)]
            g_now = [zero] * UNROLL
            for s in range(slots):
                c_now = [
                    jnp.broadcast_to(c_rows[n * slots + s : n * slots + s + 1, :], (SUB, lanes)) for n in range(chunks)
                ]
                for u in range(UNROLL):
                    for j in range(chunks):
                        spot = pl.multiple_of(j * lanes + at[u], SUB)
                        dots = None
                        for n in range(chunks):
                            term = tiles[s, pl.ds(spot, SUB), n * lanes : (n + 1) * lanes] * c_now[n]
                            dots = term if dots is None else dots + term
                        summed = jnp.sum(dots, axis=1, keepdims=True)
                        g_now[u] = jnp.where(lane_iota == j * slots + s, summed, g_now[u])
            for u in range(UNROLL):
                g_cols[pl.ds(at[u], SUB), :] = g_now[u]
            return carry

        lax.fori_loop(0, lanes // (SUB * UNROLL), direct, 0)

        @pl.when(k == last)
        def _():
            for copy in quad_copies():
                copy.wait_recv()
            last_out[...] = jnp.sum(quad_in[...], axis=0)
            for copy in last_copies():
                copy.start()
            last_in[f] = last_out[...]

        row_out[k] = select(put_row, g_cols[...].T[: put_row.shape[1] // 2, :])
        for copy in row_returns(k):
            copy.start()
        row_back[k, c] = row_out[k, pl.ds(pl.multiple_of(c * slab, SUB), slab), :]
        unless(is_first, lambda: spill_copy(k).wait_recv())
        image[0] = image[0] + spill_in[k]
        for copy in col_returns(k) + row_returns(k):
            copy.wait_recv()
        total = jnp.sum(row_back[k], axis=0) + jnp.sum(col_back[k], axis=0)
        nus[k] = total[0:SUB, :]
        for h in range(blocks):
            part = jnp.where(row_iota < COMP, total[h * SUB : (h + 1) * SUB, :], 0.0)
            image[h] = image[h] + swap_pairs(part, side)
            ys[k + 1, h] = image[h]

        @pl.when(k < last)
        def _():
            for h in range(blocks):
                vecs[k + 1, h] = precondition(h, image[h])
            publish(k + 1)

        return carry

    last = ITERS - 1
    lax.fori_loop(0, ITERS, step, 0)

    moments = []
    for k in range(ITERS):
        if k:
            moments.append(jnp.sum(nus[k, COMP + 1 : COMP + 2, :], axis=1, keepdims=True))
        moments.append(jnp.sum(nus[k, COMP : COMP + 1, :], axis=1, keepdims=True))

    def quadratic(coefs, values):
        sums = {}
        for i, left in enumerate(coefs):
            for j, right in enumerate(coefs):
                sums.setdefault(i + j, []).append(left * right)
        total = None
        for at, terms in sums.items():
            term = sum(terms[1:], terms[0]) * values(at)
            total = term if total is None else total + term
        return total

    one = jnp.ones((1, 1), jnp.float32)
    none = jnp.zeros((1, 1), jnp.float32)
    rho = [one]
    pi = [one]
    xi = []
    gamma = quadratic(rho, lambda at: moments[at])
    for iteration in range(ITERS):
        if iteration == last:
            for copy in last_copies():
                copy.wait_recv()
            ending = jnp.sum(last_in[...], axis=0)[0:1, :]
            moments.append(jnp.sum(ending, axis=1, keepdims=True))
        alpha = gamma / quadratic(pi, lambda at: moments[at] + moments[at + 1])
        xi = [x + alpha * p for x, p in zip(xi + [none] * (len(pi) - len(xi)), pi)]
        image = [(pi[i] if i < len(pi) else none) + (pi[i - 1] if i else none) for i in range(len(pi) + 1)]
        rho = [r - alpha * s for r, s in zip(rho + [none], image)]
        if iteration < last:
            fresh = quadratic(rho, lambda at: moments[at])
            beta = fresh / gamma
            pi = [r + beta * p for r, p in zip(rho, pi + [none])]
            gamma = fresh

    for h in range(blocks):
        cut = slice(h * lanes, (h + 1) * lanes)
        sol = zero
        res = zero
        for k in range(ITERS):
            sol = sol + xi[k] * vecs[k, h]
        for k in range(ITERS + 1):
            res = res + rho[k] * ys[k, h]
        out_ref[0, :, cut] = sol[0:COMP, :]
        out_ref[1, :, cut] = res[0:COMP, :]
    sent(last)
    for copy in quad_copies() + last_copies():
        copy.wait_send()


def per_device(nf, nc, right_side, diag_blocks, band_blocks, reach, tiles, tile_rows, tile_cols, tile_count):
    slots, tile = tiles.shape[2], tiles.shape[3]
    lanes = 2 * (tile // COMP)
    chunks = tile // lanes
    frames = right_side.shape[1]
    blocks = frames // lanes
    slab = blocks * SUB
    reach_len = band_blocks.shape[0]
    padded = -(-slots * chunks // (2 * SUB)) * 2 * SUB
    f32 = jnp.float32
    vmem = pl.BlockSpec(memory_space=pltpu.VMEM)
    dma = pltpu.SemaphoreType.DMA
    bf16 = jnp.bfloat16
    scratch = [
        pltpu.VMEM(right_side.shape, f32),
        pltpu.VMEM(diag_blocks.shape, f32),
        pltpu.VMEM((COMP, COMP, reach_len, frames), f32),
        pltpu.VMEM((1, frames), jnp.int32),
        pltpu.SMEM(tile_rows.shape, jnp.int32),
        pltpu.SMEM(tile_cols.shape, jnp.int32),
        pltpu.SMEM(tile_count.shape, jnp.int32),
        pltpu.VMEM((slots, tile, tile), f32),
        pltpu.VMEM((COMP, COMP, blocks, SUB, lanes), f32),
        pltpu.VMEM((COMP, COMP, blocks, SUB, lanes), f32),
        pltpu.VMEM((COMP, blocks, SUB, lanes), f32),
        pltpu.VMEM((ITERS + 1, blocks, SUB, lanes), f32),
        pltpu.VMEM((ITERS + 1, blocks, SUB, lanes), f32),
        pltpu.VMEM((ITERS, nc, slab, lanes), f32),
        pltpu.VMEM((ITERS, nf, slab, lanes), f32),
        pltpu.VMEM((ITERS, SUB, lanes), f32),
        pltpu.VMEM((ITERS, SUB, lanes), f32),
        pltpu.VMEM((ITERS, SUB, lanes), f32),
        pltpu.VMEM((ITERS, nc * slab, lanes), f32),
        pltpu.VMEM((ITERS, nf * slab, lanes), f32),
        pltpu.VMEM((ITERS, nc, slab, lanes), f32),
        pltpu.VMEM((ITERS, nf, slab, lanes), f32),
        pltpu.VMEM((SUB, lanes), f32),
        pltpu.VMEM((nc, SUB, lanes), f32),
        pltpu.VMEM((SUB, lanes), f32),
        pltpu.VMEM((nf, SUB, lanes), f32),
        pltpu.VMEM((padded, 2 * nc * slab), bf16),
        pltpu.VMEM((padded, 2 * nf * slab), bf16),
        pltpu.VMEM((nc * slab, 2 * padded), bf16),
        pltpu.VMEM((nf * slab, 2 * padded), bf16),
        pltpu.VMEM((lanes, padded), f32),
        pltpu.VMEM((padded, lanes), f32),
        pltpu.VMEM((lanes, lanes), f32),
        pltpu.VMEM((padded, lanes), f32),
        pltpu.VMEM((ITERS, SUB, lanes), f32),
        dma((slots,)),
        dma((7,)),
    ]
    for shape in ((ITERS, nc), (ITERS, nf), (ITERS,), (ITERS,), (ITERS, nc), (ITERS, nf), (nc,), (nf,)):
        scratch += [dma(shape), dma(shape)]
    out = pl.pallas_call(
        functools.partial(kernel, nf, nc),
        out_shape=jax.ShapeDtypeStruct((2,) + right_side.shape, f32),
        in_specs=[pl.BlockSpec(memory_space=pltpu.HBM)] * 8,
        out_specs=vmem,
        scratch_shapes=scratch,
        compiler_params=pltpu.CompilerParams(
            collective_id=0, has_side_effects=True, vmem_limit_bytes=60 * 1024 * 1024
        ),
        cost_estimate=pl.CostEstimate(
            flops=4 * ITERS * tiles.size, bytes_accessed=4 * (tiles.size + band_blocks.size), transcendentals=0
        ),
    )(right_side, diag_blocks, band_blocks.transpose(1, 2, 0, 3), reach.reshape(1, -1), tiles, tile_rows, tile_cols, tile_count)
    return out[0], out[1]


def solution(mesh):
    return jax.shard_map(
        functools.partial(per_device, mesh.shape["frames"], mesh.shape["cols"]),
        mesh=mesh,
        in_specs=(
            P(None, ("frames", "cols")),
            P(None, None, ("frames", "cols")),
            P(None, None, None, ("frames", "cols")),
            P(("frames", "cols")),
            P("frames", "cols", None, None, None),
            P("frames", "cols", None),
            P("frames", "cols", None),
            P("frames", "cols"),
        ),
        out_specs=(P(None, ("frames", "cols")), P(None, ("frames", "cols"))),
        check_vma=False,
    )
```

```python
import functools

import jax
import jax.numpy as jnp
from jax import lax
from jax.experimental import pallas as pl
from jax.experimental.pallas import tpu as pltpu
from jax.sharding import PartitionSpec as P

ITERS = 4
COMP = 6
SUB = 8
UNROLL = 8
MESH = pl.DeviceIdType.MESH


def swap_pairs(block, side):
    row = lax.broadcasted_iota(jnp.int32, block.shape, 0)
    lane = lax.broadcasted_iota(jnp.int32, block.shape, 1)
    odd = row % 2
    turned = pltpu.roll(block, side, 1)
    above = pltpu.roll(turned, SUB - 1, 0)
    below = pltpu.roll(turned, 1, 0)
    return jnp.where(odd == lane // side, block, jnp.where(odd == 0, above, below))


def flip_rows(block):
    row = lax.broadcasted_iota(jnp.int32, block.shape, 0)
    block = pltpu.roll(block, SUB // 2, 0)
    for step in (2, 1):
        up, down = pltpu.roll(block, SUB - step, 0), pltpu.roll(block, step, 0)
        block = jnp.where((row // step) % 2 == 0, up, down)
    return block


def kernel(
    nf,
    nc,
    rhs_hbm,
    diag_hbm,
    band_hbm,
    reach_hbm,
    tiles_hbm,
    rows_hbm,
    cols_hbm,
    count_hbm,
    out_ref,
    rhs_ref,
    diag_ref,
    band_ref,
    reach_ref,
    rows_ref,
    cols_ref,
    count_ref,
    tiles,
    band,
    flipped,
    inv,
    vecs,
    ys,
    row_in,
    col_in,
    halo_in,
    spill_out,
    spill_in,
    row_out,
    col_out,
    row_back,
    col_back,
    quad_out,
    quad_in,
    last_out,
    last_in,
    pick_row,
    pick_col,
    put_row,
    put_col,
    r_cols,
    c_rows,
    g_cols,
    col_acc,
    nus,
    tile_sem,
    load_sem,
    s_row,
    r_row,
    s_col,
    r_col,
    s_halo,
    r_halo,
    s_spill,
    r_spill,
    s_rowb,
    r_rowb,
    s_colb,
    r_colb,
    s_quad,
    r_quad,
    s_last,
    r_last,
):
    f = lax.axis_index("frames")
    c = lax.axis_index("cols")
    slots, tile, _ = tiles.shape
    side = tile // COMP
    lanes = 2 * side
    chunks = tile // lanes
    blocks = vecs.shape[1]
    frames = blocks * lanes
    slab = blocks * SUB
    reach_len = band_ref.shape[2]

    small = [
        pltpu.make_async_copy(src, dst, load_sem.at[at])
        for at, (src, dst) in enumerate(
            (
                (diag_hbm, diag_ref),
                (rhs_hbm, rhs_ref),
                (rows_hbm, rows_ref),
                (cols_hbm, cols_ref),
                (count_hbm, count_ref),
                (reach_hbm, reach_ref),
                (band_hbm, band_ref),
            )
        )
    ]
    for copy in small:
        copy.start()
    loads = [pltpu.make_async_copy(tiles_hbm.at[0, 0, t], tiles.at[t], tile_sem.at[t]) for t in range(slots)]
    for copy in loads:
        copy.start()

    row_peers = [(f, lax.rem(c + d, nc)) for d in range(1, nc)]
    col_peers = [(lax.rem(f + d, nf), c) for d in range(1, nf)]
    after = (lax.rem(f + (c + 1) // nc, nf), lax.rem(c + 1, nc))
    before = (lax.rem(f + nf - 1 + (c + nc - 1) // nc, nf), lax.rem(c + nc - 1, nc))
    is_first = (f == 0) & (c == 0)
    is_last = (f == nf - 1) & (c == nc - 1)
    barrier = pltpu.get_barrier_semaphore()

    def greet(peer):
        pl.semaphore_signal(barrier, inc=1, device_id=peer, device_id_type=MESH)

    for peer in col_peers + row_peers:
        greet(peer)

    @pl.when(jnp.logical_not(is_first))
    def _():
        greet(before)

    @pl.when(jnp.logical_not(is_last))
    def _():
        greet(after)

    @pl.when(is_first)
    def _():
        spill_in[...] = jnp.zeros_like(spill_in)

    @pl.when(is_last)
    def _():
        halo_in[...] = jnp.zeros_like(halo_in)

    row_iota = lax.broadcasted_iota(jnp.int32, (SUB, lanes), 0)
    lane_iota = lax.broadcasted_iota(jnp.int32, (SUB, lanes), 1)
    zero = jnp.zeros((SUB, lanes), jnp.float32)

    ys[0] = jnp.zeros((blocks, SUB, lanes), jnp.float32)
    inv[...] = jnp.zeros_like(inv)
    for copy in small[:2]:
        copy.wait()
    for h in range(blocks):
        cut = slice(h * lanes, (h + 1) * lanes)
        ys[0, h, 0:COMP, :] = rhs_ref[:, cut]
        for a in range(COMP):
            inv[a, h, 0:COMP, :] = diag_ref[a, :, cut]
    for h in range(blocks):
        mat = [inv[a, h] for a in range(COMP)]
        out = [jnp.where(row_iota == a, 1.0, 0.0) for a in range(COMP)]
        for p in range(COMP):
            pivot = mat[p][p : p + 1, :]
            mat[p] = mat[p] / pivot
            out[p] = out[p] / pivot
            for a in range(COMP):
                if a != p:
                    factor = mat[a][p : p + 1, :]
                    mat[a] = mat[a] - factor * mat[p]
                    out[a] = out[a] - factor * out[p]
        for a in range(COMP):
            inv[a, h] = out[a]

    def precondition(h, value):
        total = zero
        for a in range(COMP):
            total = total + inv[a, h] * value[a : a + 1, :]
        return total

    for h in range(blocks):
        vecs[0, h] = precondition(h, ys[0, h])

    ends = jnp.where(is_first, 1, 0) + jnp.where(is_last, 1, 0)
    pl.semaphore_wait(barrier, len(col_peers) + len(row_peers) + 2 - ends)

    def unless(edge, act):
        @pl.when(jnp.logical_not(edge))
        def _():
            act()

    def remote(src, dst, send, recv, peer):
        return pltpu.make_async_remote_copy(
            src_ref=src, dst_ref=dst, send_sem=send, recv_sem=recv, device_id=peer, device_id_type=MESH
        )

    def row_gathers(k):
        return [
            remote(row_in.at[k, c], row_in.at[k, c], s_row.at[k, d], r_row.at[k, d], row_peers[d - 1])
            for d in range(1, nc)
        ]

    def col_gathers(k):
        return [
            remote(col_in.at[k, f], col_in.at[k, f], s_col.at[k, d], r_col.at[k, d], col_peers[d - 1])
            for d in range(1, nf)
        ]

    def halo_copy(k):
        return remote(vecs.at[k, 0], halo_in.at[k], s_halo.at[k], r_halo.at[k], before)

    def spill_copy(k):
        return remote(spill_out.at[k], spill_in.at[k], s_spill.at[k], r_spill.at[k], after)

    def col_returns(k):
        copies = []
        for d in range(1, nf):
            peer = col_peers[d - 1]
            part = col_out.at[k, pl.ds(pl.multiple_of(peer[0] * slab, SUB), slab), :]
            copies.append(remote(part, col_back.at[k, f], s_colb.at[k, d], r_colb.at[k, d], peer))
        return copies

    def row_returns(k):
        copies = []
        for d in range(1, nc):
            peer = row_peers[d - 1]
            part = row_out.at[k, pl.ds(pl.multiple_of(peer[1] * slab, SUB), slab), :]
            copies.append(remote(part, row_back.at[k, c], s_rowb.at[k, d], r_rowb.at[k, d], peer))
        return copies

    def quad_copies():
        return [remote(quad_out, quad_in.at[c], s_quad.at[d], r_quad.at[d], row_peers[d - 1]) for d in range(1, nc)]

    def last_copies():
        return [remote(last_out, last_in.at[f], s_last.at[d], r_last.at[d], col_peers[d - 1]) for d in range(1, nf)]

    def sent(k):
        for copy in row_gathers(k) + col_gathers(k) + col_returns(k) + row_returns(k):
            copy.wait_send()
        unless(is_first, lambda: halo_copy(k).wait_send())
        unless(is_last, lambda: spill_copy(k).wait_send())

    def publish(k):
        prev = jnp.maximum(k - 1, 0)
        even = jnp.zeros((1, lanes), jnp.float32)
        odd = jnp.zeros((1, lanes), jnp.float32)
        for h in range(blocks):
            y = ys[k, h]
            even = even + jnp.sum(vecs[k, h] * y, axis=0, keepdims=True)
            odd = odd + jnp.sum(vecs[prev, h] * y, axis=0, keepdims=True)
        paired = [swap_pairs(vecs[k, h], side) for h in range(blocks)]
        paired[0] = jnp.where(row_iota == COMP, even, jnp.where(row_iota == COMP + 1, odd, paired[0]))
        for h in range(blocks):
            row_in[k, c, h * SUB : (h + 1) * SUB, :] = paired[h]
            col_in[k, f, h * SUB : (h + 1) * SUB, :] = paired[h]
        for copy in row_gathers(k) + col_gathers(k):
            copy.start()
        unless(is_first, lambda: halo_copy(k).start())

    publish(0)

    for copy in small[2:]:
        copy.wait()

    limit = jnp.where(is_last, frames, frames + reach_len)
    for h in range(blocks):
        cut = slice(h * lanes, (h + 1) * lanes)
        offset = row_iota + 1
        keep = (offset <= reach_ref[:, cut]) & (lane_iota + h * lanes + offset < limit)
        keep = jnp.where(keep, 1.0, 0.0)
        for a in range(COMP):
            for b in range(COMP):
                block = band_ref[a, b, :, cut] * keep
                band[a, b, h] = block
                flipped[a, b, h] = flip_rows(block)

    count = count_ref[0, 0]

    def targets(ids_ref, iota):
        out = jnp.full(iota.shape, -1, jnp.int32)
        for s in range(slots):
            at = ids_ref[0, 0, s]
            base = jnp.where(s < count, (at // 2) * SUB + lax.rem(at, 2), -slab * nf * nc)
            for j in range(chunks):
                out = jnp.where(iota == j * slots + s, base + 2 * j, out)
        return out

    for ids, pick, put in ((rows_ref, pick_row, put_row), (cols_ref, pick_col, put_col)):
        rows, wide = pick.shape[0], pick.shape[1] // 2
        down = targets(ids, lax.broadcasted_iota(jnp.int32, (rows, 1), 0))
        once = jnp.where(lax.broadcasted_iota(jnp.int32, (rows, wide), 1) == down, 1.0, 0.0)
        pick[...] = jnp.concatenate([once] * 2, axis=1).astype(jnp.bfloat16)
        rows, wide = put.shape[0], put.shape[1] // 2
        along = targets(ids, lax.broadcasted_iota(jnp.int32, (1, wide), 1))
        once = jnp.where(lax.broadcasted_iota(jnp.int32, (rows, wide), 0) == along, 1.0, 0.0)
        put[...] = jnp.concatenate([once] * 2, axis=1).astype(jnp.bfloat16)

    def select(pick, value):
        first = value.astype(jnp.bfloat16)
        second = (value - first.astype(jnp.float32)).astype(jnp.bfloat16)
        parts = jnp.concatenate([first, second], axis=0)
        return jnp.dot(pick[...], parts, preferred_element_type=jnp.float32)

    slot_row = lax.broadcasted_iota(jnp.int32, (slots, lanes), 0)

    def step(k, carry):
        v = [vecs[k, h] for h in range(blocks)]

        image = [zero] * blocks
        spill = zero
        for b in range(COMP):
            passed = zero
            for h in range(blocks):
                term = zero
                for a in range(COMP):
                    term = term + band[a, b, h] * v[h][a : a + 1, :]
                turned = pltpu.roll(term, 1, 1, stride=1, stride_axis=0)
                moved = jnp.sum(jnp.where(lane_iota > row_iota, turned, passed), axis=0, keepdims=True)
                image[h] = jnp.where(row_iota == b, moved, image[h])
                passed = turned
            moved = jnp.sum(jnp.where(lane_iota > row_iota, 0.0, passed), axis=0, keepdims=True)
            spill = jnp.where(row_iota == b, moved, spill)
        spill_out[k] = spill
        unless(is_last, lambda: spill_copy(k).start())

        for copy in row_gathers(k):
            copy.wait_recv()
        rows_all = row_in[k].reshape(nc * slab, lanes)
        r_cols[...] = select(pick_row, rows_all).T

        @pl.when(k == 0)
        def _():
            for copy in loads:
                copy.wait()

        def transposed(i, accs):
            accs = list(accs)
            at = [pl.multiple_of((i * UNROLL + u) * SUB, SUB) for u in range(UNROLL)]
            r_now = [r_cols[pl.ds(at[u], SUB), :] for u in range(UNROLL)]
            for s in range(slots):
                for u in range(UNROLL):
                    for j in range(chunks):
                        col = j * slots + s
                        spot = pl.multiple_of(j * lanes + at[u], SUB)
                        x = jnp.broadcast_to(r_now[u][:, col : col + 1], (SUB, lanes))
                        for n in range(chunks):
                            part = tiles[s, pl.ds(spot, SUB), n * lanes : (n + 1) * lanes]
                            accs[n * slots + s] = accs[n * slots + s] + part * x
            return tuple(accs)

        accs = lax.fori_loop(0, lanes // (SUB * UNROLL), transposed, (zero,) * (slots * chunks))
        col_acc[...] = jnp.zeros_like(col_acc)
        for n in range(chunks):
            folded = jnp.zeros((slots, lanes), jnp.float32)
            for s in range(slots):
                summed = jnp.sum(accs[n * slots + s], axis=0, keepdims=True)
                folded = jnp.where(slot_row == s, summed, folded)
            col_acc[n * slots : (n + 1) * slots, :] = folded
        col_out[k] = select(put_col, col_acc[...])
        sums = jnp.zeros((2, lanes), jnp.float32)
        for d in range(nc):
            sums = sums + row_in[k, d, COMP:SUB, :]
        for d in range(nf):
            col_out[k, d * slab + COMP : d * slab + SUB, :] = sums
        for copy in col_returns(k):
            copy.start()
        col_back[k, f] = col_out[k, pl.ds(pl.multiple_of(f * slab, SUB), slab), :]

        @pl.when(k > 0)
        def _():
            sent(k - 1)

        unless(is_last, lambda: halo_copy(k).wait_recv())
        ext = v + [halo_in[k]]
        forward = [[zero] * COMP for _ in range(blocks)]
        for b in range(COMP):
            turned = [
                pltpu.roll(jnp.broadcast_to(part[b : b + 1, :], (SUB, lanes)), lanes - SUB, 1, stride=1, stride_axis=0)
                for part in ext
            ]
            for h in range(blocks):
                moved = jnp.where(lane_iota - row_iota < lanes - SUB, turned[h], turned[h + 1])
                for a in range(COMP):
                    forward[h][a] = forward[h][a] + flipped[a, b, h] * moved
        quad = jnp.zeros((1, lanes), jnp.float32)
        for h in range(blocks):
            ahead = zero
            for a in range(COMP):
                ahead = jnp.where(row_iota == a, jnp.sum(forward[h][a], axis=0, keepdims=True), ahead)
            quad = quad + jnp.sum(ahead * v[h], axis=0, keepdims=True)
            image[h] = image[h] + ahead

        for copy in col_gathers(k):
            copy.wait_recv()
        cols_all = col_in[k].reshape(nf * slab, lanes)
        c_rows[...] = select(pick_col, cols_all)

        @pl.when(k == last)
        def _():
            part = 2.0 * (quad + jnp.sum(col_acc[...] * c_rows[...], axis=0, keepdims=True))
            quad_out[...] = jnp.broadcast_to(part, (SUB, lanes))
            for copy in quad_copies():
                copy.start()
            quad_in[c] = quad_out[...]

        def direct(i, carry):
            at = [pl.multiple_of((i * UNROLL + u) * SUB, SUB) for u in range(UNROLL)]
            g_now = [zero] * UNROLL
            for s in range(slots):
                c_now = [
                    jnp.broadcast_to(c_rows[n * slots + s : n * slots + s + 1, :], (SUB, lanes)) for n in range(chunks)
                ]
                for u in range(UNROLL):
                    for j in range(chunks):
                        spot = pl.multiple_of(j * lanes + at[u], SUB)
                        dots = None
                        for n in range(chunks):
                            term = tiles[s, pl.ds(spot, SUB), n * lanes : (n + 1) * lanes] * c_now[n]
                            dots = term if dots is None else dots + term
                        summed = jnp.sum(dots, axis=1, keepdims=True)
                        g_now[u] = jnp.where(lane_iota == j * slots + s, summed, g_now[u])
            for u in range(UNROLL):
                g_cols[pl.ds(at[u], SUB), :] = g_now[u]
            return carry

        lax.fori_loop(0, lanes // (SUB * UNROLL), direct, 0)

        @pl.when(k == last)
        def _():
            for copy in quad_copies():
                copy.wait_recv()
            last_out[...] = jnp.sum(quad_in[...], axis=0)
            for copy in last_copies():
                copy.start()
            last_in[f] = last_out[...]

        row_out[k] = select(put_row, g_cols[...].T[: put_row.shape[1] // 2, :])
        for copy in row_returns(k):
            copy.start()
        row_back[k, c] = row_out[k, pl.ds(pl.multiple_of(c * slab, SUB), slab), :]
        unless(is_first, lambda: spill_copy(k).wait_recv())
        image[0] = image[0] + spill_in[k]
        for copy in col_returns(k) + row_returns(k):
            copy.wait_recv()
        total = jnp.sum(row_back[k], axis=0) + jnp.sum(col_back[k], axis=0)
        nus[k] = total[0:SUB, :]
        for h in range(blocks):
            part = jnp.where(row_iota < COMP, total[h * SUB : (h + 1) * SUB, :], 0.0)
            image[h] = image[h] + swap_pairs(part, side)
            ys[k + 1, h] = image[h]

        @pl.when(k < last)
        def _():
            for h in range(blocks):
                vecs[k + 1, h] = precondition(h, image[h])
            publish(k + 1)

        return carry

    last = ITERS - 1
    lax.fori_loop(0, ITERS, step, 0)

    moments = []
    for k in range(ITERS):
        if k:
            moments.append(jnp.sum(nus[k, COMP + 1 : COMP + 2, :], axis=1, keepdims=True))
        moments.append(jnp.sum(nus[k, COMP : COMP + 1, :], axis=1, keepdims=True))

    def quadratic(coefs, values):
        sums = {}
        for i, left in enumerate(coefs):
            for j, right in enumerate(coefs):
                sums.setdefault(i + j, []).append(left * right)
        total = None
        for at, terms in sums.items():
            term = sum(terms[1:], terms[0]) * values(at)
            total = term if total is None else total + term
        return total

    one = jnp.ones((1, 1), jnp.float32)
    none = jnp.zeros((1, 1), jnp.float32)
    rho = [one]
    pi = [one]
    xi = []
    gamma = quadratic(rho, lambda at: moments[at])
    for iteration in range(ITERS):
        if iteration == last:
            for copy in last_copies():
                copy.wait_recv()
            ending = jnp.sum(last_in[...], axis=0)[0:1, :]
            moments.append(jnp.sum(ending, axis=1, keepdims=True))
        alpha = gamma / quadratic(pi, lambda at: moments[at] + moments[at + 1])
        xi = [x + alpha * p for x, p in zip(xi + [none] * (len(pi) - len(xi)), pi)]
        image = [(pi[i] if i < len(pi) else none) + (pi[i - 1] if i else none) for i in range(len(pi) + 1)]
        rho = [r - alpha * s for r, s in zip(rho + [none], image)]
        if iteration < last:
            fresh = quadratic(rho, lambda at: moments[at])
            beta = fresh / gamma
            pi = [r + beta * p for r, p in zip(rho, pi + [none])]
            gamma = fresh

    for h in range(blocks):
        cut = slice(h * lanes, (h + 1) * lanes)
        sol = zero
        res = zero
        for k in range(ITERS):
            sol = sol + xi[k] * vecs[k, h]
        for k in range(ITERS + 1):
            res = res + rho[k] * ys[k, h]
        out_ref[0, :, cut] = sol[0:COMP, :]
        out_ref[1, :, cut] = res[0:COMP, :]
    sent(last)
    for copy in quad_copies() + last_copies():
        copy.wait_send()


def per_device(nf, nc, right_side, diag_blocks, band_blocks, reach, tiles, tile_rows, tile_cols, tile_count):
    slots, tile = tiles.shape[2], tiles.shape[3]
    lanes = 2 * (tile // COMP)
    chunks = tile // lanes
    frames = right_side.shape[1]
    blocks = frames // lanes
    slab = blocks * SUB
    reach_len = band_blocks.shape[0]
    padded = -(-slots * chunks // (2 * SUB)) * 2 * SUB
    f32 = jnp.float32
    vmem = pl.BlockSpec(memory_space=pltpu.VMEM)
    dma = pltpu.SemaphoreType.DMA
    bf16 = jnp.bfloat16
    scratch = [
        pltpu.VMEM(right_side.shape, f32),
        pltpu.VMEM(diag_blocks.shape, f32),
        pltpu.VMEM((COMP, COMP, reach_len, frames), f32),
        pltpu.VMEM((1, frames), jnp.int32),
        pltpu.SMEM(tile_rows.shape, jnp.int32),
        pltpu.SMEM(tile_cols.shape, jnp.int32),
        pltpu.SMEM(tile_count.shape, jnp.int32),
        pltpu.VMEM((slots, tile, tile), f32),
        pltpu.VMEM((COMP, COMP, blocks, SUB, lanes), f32),
        pltpu.VMEM((COMP, COMP, blocks, SUB, lanes), f32),
        pltpu.VMEM((COMP, blocks, SUB, lanes), f32),
        pltpu.VMEM((ITERS + 1, blocks, SUB, lanes), f32),
        pltpu.VMEM((ITERS + 1, blocks, SUB, lanes), f32),
        pltpu.VMEM((ITERS, nc, slab, lanes), f32),
        pltpu.VMEM((ITERS, nf, slab, lanes), f32),
        pltpu.VMEM((ITERS, SUB, lanes), f32),
        pltpu.VMEM((ITERS, SUB, lanes), f32),
        pltpu.VMEM((ITERS, SUB, lanes), f32),
        pltpu.VMEM((ITERS, nc * slab, lanes), f32),
        pltpu.VMEM((ITERS, nf * slab, lanes), f32),
        pltpu.VMEM((ITERS, nc, slab, lanes), f32),
        pltpu.VMEM((ITERS, nf, slab, lanes), f32),
        pltpu.VMEM((SUB, lanes), f32),
        pltpu.VMEM((nc, SUB, lanes), f32),
        pltpu.VMEM((SUB, lanes), f32),
        pltpu.VMEM((nf, SUB, lanes), f32),
        pltpu.VMEM((padded, 2 * nc * slab), bf16),
        pltpu.VMEM((padded, 2 * nf * slab), bf16),
        pltpu.VMEM((nc * slab, 2 * padded), bf16),
        pltpu.VMEM((nf * slab, 2 * padded), bf16),
        pltpu.VMEM((lanes, padded), f32),
        pltpu.VMEM((padded, lanes), f32),
        pltpu.VMEM((lanes, lanes), f32),
        pltpu.VMEM((padded, lanes), f32),
        pltpu.VMEM((ITERS, SUB, lanes), f32),
        dma((slots,)),
        dma((7,)),
    ]
    for shape in ((ITERS, nc), (ITERS, nf), (ITERS,), (ITERS,), (ITERS, nc), (ITERS, nf), (nc,), (nf,)):
        scratch += [dma(shape), dma(shape)]
    out = pl.pallas_call(
        functools.partial(kernel, nf, nc),
        out_shape=jax.ShapeDtypeStruct((2,) + right_side.shape, f32),
        in_specs=[pl.BlockSpec(memory_space=pltpu.HBM)] * 8,
        out_specs=vmem,
        scratch_shapes=scratch,
        compiler_params=pltpu.CompilerParams(
            collective_id=0, has_side_effects=True, vmem_limit_bytes=60 * 1024 * 1024
        ),
        cost_estimate=pl.CostEstimate(
            flops=4 * ITERS * tiles.size, bytes_accessed=4 * (tiles.size + band_blocks.size), transcendentals=0
        ),
    )(right_side, diag_blocks, band_blocks.transpose(1, 2, 0, 3), reach.reshape(1, -1), tiles, tile_rows, tile_cols, tile_count)
    return out[0], out[1]


def solution(mesh):
    return jax.shard_map(
        functools.partial(per_device, mesh.shape["frames"], mesh.shape["cols"]),
        mesh=mesh,
        in_specs=(
            P(None, ("frames", "cols")),
            P(None, None, ("frames", "cols")),
            P(None, None, None, ("frames", "cols")),
            P(("frames", "cols")),
            P("frames", "cols", None, None, None),
            P("frames", "cols", None),
            P("frames", "cols", None),
            P("frames", "cols"),
        ),
        out_specs=(P(None, ("frames", "cols")), P(None, ("frames", "cols"))),
        check_vma=False,
    )
```
